128 devices in a mesh: ctx: 32 (over x, z, y_hi), head: 4 (over y_lo, core).
Axes of the slice: x: 4, y: 4 (y_hi: 2, y_lo: 2; y = y_hi * 2 + y_lo), z: 4, core: 2. Of those that a mesh axis runs over, the one named last changes fastest.
Arguments:
- query: bfloat16 [16384, 8192], P(('ctx', 'head')), may hold values from -6 to 6
- key: bfloat16 [16384, 1024], P(('ctx', 'head')), may hold values from -12 to 12
- value: bfloat16 [16384, 1024], P(('ctx', 'head')), may hold values from -6 to 6
- grad_out: bfloat16 [16384, 8192], P(('ctx', 'head')), may hold values from -6 to 6
- advantage: float32 [16384], P(('ctx', 'head')), may hold values from -3 to 3
- place: int32 [16384], replicated, may hold values from 0 to 16383, as said below
- segment: int32 [16384], replicated, may hold values from 0 to 93, as said below
Outputs:
- grad_query: bfloat16 [16384, 8192], P(('ctx', 'head'))
- grad_key: bfloat16 [16384, 1024], P(('ctx', 'head'))
- grad_value: bfloat16 [16384, 1024], P(('ctx', 'head'))
The draws below stay inside these ranges and needn't reach their ends.
Inputs may be any that keep to these rules, and one draw needn't show every extreme that they name: place is a permutation; each aligned block of 128 tokens sends exactly 4 tokens to each aligned block of 512 positions. segment never falls along positions and starts at 0; each document holds 2 to 512 positions, and one holds exactly 512.
All inputs are finite; a program needn't handle non-finite values.
Results may differ from the reference program's by a relative error of at most 0.0066.
Values may be sent and summed in bfloat16 or wider, within the bound.
No kernel may reach another device: no remote copies, remote signals or barrier semaphores. Data moves between devices by JAX's collectives and lax.ppermute only.
A program may use at most 128 MiB of HBM per device.

```python
import jax
import jax.numpy as jnp
from jax import lax

QUERY_HEADS = 64
KEY_VALUE_HEADS = 8
HEAD_SIZE = 128
TOK_DEV = 512
SRC_ROWS = 128
SENT = 4
PACKED_TOKENS = 16384
N_CTX = 32
DEVICES = 128


def layout_tables(key):
    source_keys = jax.random.split(jax.random.fold_in(key, 11), DEVICES)
    local_perm = jax.vmap(lambda piece_key: jax.random.permutation(piece_key, SRC_ROWS))(source_keys)
    dest_block = (local_perm // SENT).reshape(PACKED_TOKENS).astype(jnp.int32)
    shuffle = jax.random.permutation(jax.random.fold_in(key, 12), PACKED_TOKENS).astype(jnp.int32)
    order = jnp.argsort(dest_block * PACKED_TOKENS + shuffle, stable=True).astype(jnp.int32)
    place = jnp.zeros((PACKED_TOKENS,), jnp.int32).at[order].set(jnp.arange(PACKED_TOKENS, dtype=jnp.int32))
    half = TOK_DEV // 2
    slabs = PACKED_TOKENS // half
    first = jax.random.randint(jax.random.fold_in(key, 14), (), 2, half - 1).astype(jnp.int32)
    joined = jax.random.randint(jax.random.fold_in(key, 15), (), 1, slabs - 5).astype(jnp.int32)
    extra_at = jax.random.randint(jax.random.fold_in(key, 16), (slabs,), 2, half - 1).astype(jnp.int32)
    slab_ids = jnp.arange(slabs, dtype=jnp.int32)
    eligible = (slab_ids != joined) & (slab_ids != joined - 1) & (slab_ids != slabs - 1)
    slab_rank = jax.random.permutation(jax.random.fold_in(key, 17), slabs).astype(jnp.int32)
    slab_score = jnp.where(eligible, slab_rank, slabs + slab_rank).astype(jnp.int32)
    slab_order = jnp.argsort(slab_score, stable=True).astype(jnp.int32)
    slab_pos = jnp.zeros((slabs,), jnp.int32).at[slab_order].set(slab_ids)
    coin = (slab_pos < (slabs - 3) // 2).astype(jnp.int32)
    positions = jnp.arange(PACKED_TOKENS, dtype=jnp.int32)
    offset = positions - first
    slab = jnp.clip(offset // half, 0, slabs - 1)
    inside = (offset >= 0) & (positions <= PACKED_TOKENS - 2)
    base_offset = inside & (offset % half == 0) & (slab != joined)
    extra = inside & (coin[slab] == 1) & (offset % half == extra_at[slab])
    segment = jnp.cumsum((base_offset | extra).astype(jnp.int32)).astype(jnp.int32)
    return (place, segment)


def draw_place(key, part):
    return layout_tables(key)[0]


def draw_segment(key, part):
    return layout_tables(key)[1]


def draw_query(key, part):
    base_offset = jnp.clip(jax.random.normal(jax.random.fold_in(key, 21), (PACKED_TOKENS, QUERY_HEADS * HEAD_SIZE), jnp.float32), -4.0, 4.0)
    return base_offset.astype(jnp.bfloat16)


def draw_key(key, part):
    row_scaling = jnp.exp(jax.random.uniform(jax.random.fold_in(key, 23), (PACKED_TOKENS, 1), jnp.float32, jnp.log(0.3), jnp.log(3.0)))
    base_offset = jnp.clip(jax.random.normal(jax.random.fold_in(key, 24), (PACKED_TOKENS, KEY_VALUE_HEADS * HEAD_SIZE), jnp.float32), -4.0, 4.0) * row_scaling
    return base_offset.astype(jnp.bfloat16)


def steps_of(rng, shape, cuts, smallest, high):
    loudness, own = 1.0, jax.random.fold_in(rng, 6)
    for axis_at, parts in cuts:
        steps = jnp.exp(jax.random.uniform(jax.random.fold_in(own, axis_at), (parts,), jnp.float32, smallest / len(cuts), high / len(cuts)))
        loudness = loudness * jnp.repeat(steps, shape[axis_at] // parts).reshape([-1 if axis == axis_at else 1 for axis in range(len(shape))])
    return loudness


def bell_draw(rng, extent, spread, limit, cuts=(), kind=jnp.bfloat16):
    drawn = spread * jax.random.normal(rng, extent, jnp.float32)
    if cuts:
        drawn = drawn * steps_of(rng, extent, cuts, -0.22, 0.18)
    return jnp.clip(drawn, -limit, limit).astype(kind)


def setup_inputs(seed: int = 0) -> dict:
    streams_of = jax.random.split(jax.random.key(seed), 8)
    return {
        "query": draw_query(jax.random.fold_in(streams_of[7], 71), 0),
        "key": draw_key(jax.random.fold_in(streams_of[7], 71), 0),
        "value": bell_draw(streams_of[2], (PACKED_TOKENS, KEY_VALUE_HEADS * HEAD_SIZE), 1.0, 6.0, ((0, 128),)),
        "grad_out": bell_draw(streams_of[3], (PACKED_TOKENS, QUERY_HEADS * HEAD_SIZE), 1.0, 6.0, ((0, 128),)),
        "advantage": bell_draw(streams_of[4], (PACKED_TOKENS,), 1.0, 3.0, ((0, 128),), jnp.float32),
        "place": draw_place(jax.random.fold_in(streams_of[7], 71), 0),
        "segment": draw_segment(jax.random.fold_in(streams_of[7], 71), 0),
    }


def reference(query, key, value, grad_out, advantage, place, segment):
    every_token = query.shape[0]
    token_per_device = every_token // N_CTX
    group_width = QUERY_HEADS // KEY_VALUE_HEADS
    score_scale = HEAD_SIZE ** -0.5
    weighted = (advantage[:, None] * grad_out.astype(jnp.float32)).astype(jnp.bfloat16)
    tok_of_pos = jnp.zeros((every_token,), jnp.int32).at[place].set(jnp.arange(every_token, dtype=jnp.int32))
    query_position = query[tok_of_pos]
    weighted_position = weighted[tok_of_pos]
    blank_fill = jnp.zeros((token_per_device, KEY_VALUE_HEADS * HEAD_SIZE), jnp.bfloat16)
    key_padding = jnp.concatenate([blank_fill, key[tok_of_pos]], axis=0)
    value_padding = jnp.concatenate([blank_fill, value[tok_of_pos]], axis=0)

    def one_block(block):
        start_offset = (block * token_per_device).astype(jnp.int32)
        query_matrix = lax.dynamic_slice_in_dim(query_position, start_offset, token_per_device, 0).astype(jnp.float32).reshape(token_per_device, KEY_VALUE_HEADS, group_width, HEAD_SIZE)
        weight_matrix = lax.dynamic_slice_in_dim(weighted_position, start_offset, token_per_device, 0).astype(jnp.float32).reshape(token_per_device, KEY_VALUE_HEADS, group_width, HEAD_SIZE)
        key_matrix = lax.dynamic_slice_in_dim(key_padding, start_offset, 2 * token_per_device, 0).astype(jnp.float32).reshape(2 * token_per_device, KEY_VALUE_HEADS, HEAD_SIZE)
        value_matrix = lax.dynamic_slice_in_dim(value_padding, start_offset, 2 * token_per_device, 0).astype(jnp.float32).reshape(2 * token_per_device, KEY_VALUE_HEADS, HEAD_SIZE)
        q_place = start_offset + jnp.arange(token_per_device, dtype=jnp.int32)
        k_place = start_offset - token_per_device + jnp.arange(2 * token_per_device, dtype=jnp.int32)
        q_doc = segment[q_place]
        k_doc = jnp.where(k_place >= 0, segment[jnp.clip(k_place, 0, every_token - 1)], -2)
        visible = (q_doc[:, None] == k_doc[None, :]) & (k_place[None, :] <= q_place[:, None])
        scores = jnp.einsum("qhgd,khd->hgqk", query_matrix, key_matrix) * score_scale
        row_high = jnp.max(jnp.where(visible, scores, -jnp.inf), axis=-1)
        row_total = jnp.sum(jnp.where(visible, jnp.exp(scores - row_high[..., None]), 0.0), axis=-1)
        row_lse = row_high + jnp.log(row_total)
        prob = jnp.where(visible, jnp.exp(scores - row_lse[..., None]), 0.0)
        token_weights = prob.astype(jnp.bfloat16).astype(jnp.float32)
        attended = jnp.einsum("hgqk,khd->qhgd", token_weights, value_matrix)
        row_delta = jnp.transpose(jnp.sum(weight_matrix * attended, axis=-1), (1, 2, 0))
        dprob = jnp.einsum("qhgd,khd->hgqk", weight_matrix, value_matrix)
        score_gradient = (prob * (dprob - row_delta[..., None]) * score_scale).astype(jnp.bfloat16).astype(jnp.float32)
        grad_q = jnp.einsum("hgqk,khd->qhgd", score_gradient, key_matrix).reshape(token_per_device, QUERY_HEADS * HEAD_SIZE).astype(jnp.bfloat16)
        key_gradient = jnp.einsum("umat,aumi->tui", score_gradient, query_matrix).reshape(2 * token_per_device, KEY_VALUE_HEADS * HEAD_SIZE)
        value_gradient = jnp.einsum("umat,aumi->tui", token_weights, weight_matrix).reshape(2 * token_per_device, KEY_VALUE_HEADS * HEAD_SIZE)
        return grad_q, key_gradient, value_gradient

    all_q, all_k, all_v = lax.map(one_block, jnp.arange(N_CTX, dtype=jnp.int32))

    def fold_halves(term_values):
        later_tokens = jnp.concatenate([term_values[1:, :token_per_device], jnp.zeros((1, token_per_device, KEY_VALUE_HEADS * HEAD_SIZE), term_values.dtype)], axis=0)
        return (term_values[:, token_per_device:] + later_tokens).reshape(every_token, KEY_VALUE_HEADS * HEAD_SIZE).astype(jnp.bfloat16)

    grad_query_pos = all_q.reshape(every_token, QUERY_HEADS * HEAD_SIZE)
    return grad_query_pos[place], fold_halves(all_k)[place], fold_halves(all_v)[place]
```

```python
import functools

import jax
import jax.numpy as jnp
from jax import lax
from jax.experimental import pallas as pl
from jax.experimental.pallas import tpu as pltpu
from jax.sharding import PartitionSpec as P

GROUPS = 8
WIDTH = 8
D = 128
BLOCK = 512
PAIRS = 16
SCALE = D ** (-0.5)
LOG2E = 1.4426950408889634
NEG = -1e30
F32 = jnp.float32
BF16 = jnp.bfloat16

SEND_ROWS = 152
BACK_ROWS = 88
VMEM_LIMIT = 56 * 1024 * 1024


def iota(shape, dim):
    return lax.broadcasted_iota(jnp.int32, shape, dim)


def dot(a, b):
    return jnp.dot(a, b, preferred_element_type=F32)


def dot_nt(a, b):
    return lax.dot_general(a, b, (((1,), (1,)), ((), ())), preferred_element_type=F32)


def spread(row):
    square = jnp.broadcast_to(row.astype(F32), (128, 128))
    return square, jnp.transpose(square)


def token_codes(place_ref, me):
    row = place_ref[pl.ds(me, 1), :]
    dest = lax.shift_right_logical(row, 9)
    across, down = spread(dest)
    before = (across == down) & (iota((128, 128), 0) < iota((128, 128), 1))
    rank = jnp.sum(before.astype(F32), axis=0, keepdims=True).astype(jnp.int32)
    return lax.shift_right_logical(dest, 1), dest & 1, rank


def row_codes(pair, half, rank, per_pair):
    first = jnp.where(half == 0, pair * per_pair + rank, -1000)
    second = jnp.where(half == 1, pair * per_pair + rank, -1000)
    halo = jnp.where((half == 1) & (pair < PAIRS - 1), (pair + 1) * per_pair + rank, -1000)
    return first, second, halo


def onehot(index, code):
    return (index == code).astype(F32).astype(BF16)


def send_kernel(me_ref, place_ref, adv_ref, q_ref, k_ref, v_ref, g_ref, out_ref, t1, t2, t3, t4, adv):
    @pl.when(pl.program_id(0) == 0)
    def _():
        pair, half, rank = token_codes(place_ref, me_ref[0])
        first, second, halo = row_codes(pair, half, rank, 16)
        rows = iota((256, 128), 0)
        for j in range(4):
            cols = slice(j * 128, (j + 1) * 128)
            t1[:, cols] = onehot(rows, first + 4 * j)
            t2[:, cols] = onehot(rows, second + 4 * j)
            t3[:, cols] = onehot(rows, (halo if j < 2 else first) + 4 * j)
        second8 = row_codes(pair, half, rank, 8)[1]
        rows8 = iota((128, 128), 0)
        for j in range(2):
            t4[:, j * 128 : (j + 1) * 128] = onehot(rows8, second8 + 4 * j)
        adv[...] = jnp.transpose(jnp.broadcast_to(adv_ref[...], (128, 128)))

    weight = adv[...]
    grad = jnp.concatenate(
        [
            (g_ref[:, h * 128 : (h + 1) * 128].astype(F32) * weight).astype(BF16)
            for h in range(WIDTH)
        ],
        axis=1,
    )
    for at, block in ((0, q_ref[...]), (64, grad)):
        stacked = jnp.concatenate([block[:, j * 256 : (j + 1) * 256] for j in range(4)], axis=0)
        for b, t in enumerate((t1, t2)):
            moved = dot(t[...], stacked).astype(BF16)
            start = at + 32 * b
            out_ref[:, 0, start : start + 16, :] = moved[:, :128].reshape(PAIRS, 16, 128)
            out_ref[:, 0, start + 16 : start + 32, :] = moved[:, 128:].reshape(PAIRS, 16, 128)
    k, v = k_ref[...], v_ref[...]
    moved = dot(t3[...], jnp.concatenate([k, v, k, v], axis=0)).astype(BF16)
    out_ref[:, 0, 128:144, :] = moved.reshape(PAIRS, 16, 128)
    moved = dot(t4[...], jnp.concatenate([k, v], axis=0)).astype(BF16)
    out_ref[:, 0, 144:152, :] = moved.reshape(PAIRS, 8, 128)


def source_maps(place_ref, block, spread_ref, gather_ref):
    place = place_ref[...]
    own = lax.shift_right_logical(place, 9) == block
    local = (place - block * BLOCK + 1).astype(F32)
    member = own.astype(F32)
    lower = (iota((128, 128), 0) < iota((128, 128), 1)).astype(F32).astype(BF16)
    rank = dot(member.astype(BF16), lower)
    picked = jnp.where(own, local, 0.0)
    member_t, picked_t = jnp.transpose(member), jnp.transpose(picked)
    upper = (iota((128, 128), 1) < iota((128, 128), 0)).astype(F32).astype(BF16)
    rank_t = dot(upper, member_t.astype(BF16))
    for r in range(4):
        col = jnp.sum(jnp.where(rank == r, picked, 0.0), axis=1, keepdims=True) - 1.0
        row = jnp.sum(jnp.where(rank_t == r, picked_t, 0.0), axis=0, keepdims=True) - 1.0
        at = slice(r * 128, (r + 1) * 128)
        spread_ref[:, at] = onehot(iota((BLOCK, 128), 0), row.astype(jnp.int32))
        gather_ref[at, :] = onehot(iota((128, BLOCK), 1), col.astype(jnp.int32))


def attend_kernel(
    me_ref, seg_ref, place_ref, doc_ref, in_ref, out_ref,
    to_pos, to_src, stage, qs, ws, ks, vs, kt, doc_t, s_scr, p_scr, dq_acc, dq_t, dk_acc, dv_acc,
):
    pair = lax.shift_right_logical(me_ref[0], 3)

    for b in range(3):
        source_maps(place_ref, 2 * pair - 1 + b, to_pos.at[b], to_src.at[b])

    def unpacked(start, rows):
        block = in_ref[:, start : start + rows, :].astype(F32)
        stage[0 : 128 * rows, :] = block.reshape(128 * rows, 128)
        return [
            jnp.concatenate(
                [stage[pl.ds(4 * j + r, 128, stride=rows), :].astype(BF16) for r in range(4)], axis=0
            )
            for j in range(rows // 4)
        ]

    for at, target in ((0, qs), (64, ws)):
        for b in range(2):
            left = unpacked(at + 32 * b, 16)
            right = unpacked(at + 32 * b + 16, 16)
            for j in range(4):
                both = jnp.concatenate([left[j], right[j]], axis=1)
                moved = dot(to_pos[b + 1], both).astype(BF16)
                target[2 * j, b * BLOCK : (b + 1) * BLOCK, :] = moved[:, :128]
                target[2 * j + 1, b * BLOCK : (b + 1) * BLOCK, :] = moved[:, 128:]
    kv = unpacked(128, 16) + unpacked(144, 8)
    for b in range(3):
        moved = dot(to_pos[b], jnp.concatenate(kv[2 * b : 2 * b + 2], axis=1)).astype(BF16)
        ks[b * BLOCK : (b + 1) * BLOCK, :] = moved[:, :128]
        vs[b * BLOCK : (b + 1) * BLOCK, :] = moved[:, 128:]
    eye = onehot(iota((128, 128), 0), iota((128, 128), 1))
    kt[...] = dot_nt(eye, ks[...]).astype(BF16)
    for b in range(12):
        at = jnp.maximum(8 * pair - 4 + b, 0)
        doc_t[b] = jnp.transpose(jnp.broadcast_to(doc_ref[pl.ds(at, 1), :].astype(F32), (128, 128)))
    dk_acc[...] = jnp.zeros_like(dk_acc)
    dv_acc[...] = jnp.zeros_like(dv_acc)

    causal = iota((128, 128), 0) - iota((128, 128), 1)

    def query_block(ib, carry):
        block = 8 * pair + ib
        first_doc = seg_ref[block * 128]
        count = jnp.int32(1)
        for back in range(1, 5):
            other = jnp.maximum(block - back, 0)
            near = (block >= back) & (seg_ref[other * 128 + 127] >= first_doc)
            count = count + near.astype(jnp.int32)
        query_doc = doc_ref[pl.ds(block, 1), :].astype(F32)
        rows = pl.ds(pl.multiple_of(ib * 128, 128), 128)

        def key_rows(t):
            return pl.ds(pl.multiple_of((ib + 4 - t) * 128, 128), 128)

        def scores(t, high):
            keys = ks[key_rows(t), :]
            seen = (doc_t[ib + 4 - t] == query_doc) & (causal <= t * 128)
            bias = jnp.where(seen, 0.0, NEG)
            new = []
            for h in range(WIDTH):
                part = dot_nt(keys, qs[h, rows, :]) * (SCALE * LOG2E) + bias
                s_scr[t, h] = part
                new.append(jnp.maximum(high[h], jnp.max(part.reshape(16, 8, 128), axis=0)))
            return tuple(new)

        high = lax.fori_loop(0, count, scores, (jnp.full((8, 128), NEG, F32),) * WIDTH)
        high = [jnp.max(x, axis=0, keepdims=True) for x in high]

        def sums(t, carry):
            total, delta = carry
            values = vs[key_rows(t), :]
            new_total, new_delta = [], []
            for h in range(WIDTH):
                prob = jnp.exp2(s_scr[t, h] - high[h])
                dprob = dot_nt(values, ws[h, rows, :])
                s_scr[t, h] = prob
                p_scr[t, h] = dprob
                new_total.append(total[h] + jnp.sum(prob.reshape(16, 8, 128), axis=0))
                new_delta.append(delta[h] + jnp.sum((prob * dprob).reshape(16, 8, 128), axis=0))
            return tuple(new_total), tuple(new_delta)

        zero = (jnp.zeros((8, 128), F32),) * WIDTH
        total, delta = lax.fori_loop(0, count, sums, (zero, zero))
        inverse = [1.0 / jnp.sum(x, axis=0, keepdims=True) for x in total]
        delta = [jnp.sum(x, axis=0, keepdims=True) * i for x, i in zip(delta, inverse)]
        dq_acc[...] = jnp.zeros_like(dq_acc)

        def grads(t, carry):
            weights, dscore = [], []
            for h in range(WIDTH):
                prob = s_scr[t, h] * inverse[h]
                weights.append(prob.astype(BF16))
                dscore.append((prob * (p_scr[t, h] - delta[h])).astype(BF16))
            weights = jnp.concatenate(weights, axis=1)
            dscore = jnp.concatenate(dscore, axis=1)
            at = key_rows(t)
            grad_rows = jnp.concatenate([ws[h, rows, :] for h in range(WIDTH)], axis=0)
            query_rows = jnp.concatenate([qs[h, rows, :] for h in range(WIDTH)], axis=0)
            dv_acc[at, :] += dot(weights, grad_rows)
            dk_acc[at, :] += dot(dscore, query_rows)
            dq_acc[...] += dot(kt[:, at], dscore)
            return carry

        lax.fori_loop(0, count, grads, 0)
        for h in range(WIDTH):
            dq_t[h, :, rows] = (dq_acc[:, h * 128 : (h + 1) * 128] * SCALE).astype(BF16)
        return carry

    lax.fori_loop(0, 8, query_block, 0)

    def packed(start, parts):
        rows = 4 * len(parts)
        for j, part in enumerate(parts):
            for r in range(4):
                stage[pl.ds(4 * j + r, 128, stride=rows), :] = part[r * 128 : (r + 1) * 128]
        out_ref[:, start : start + rows, :] = (
            stage[0 : 128 * rows, :].astype(BF16).reshape(128, rows, 128)
        )

    for b in range(2):
        for q in range(2):
            parts = [
                dot_nt(to_src[b + 1], dq_t[2 * j + q, :, b * BLOCK : (b + 1) * BLOCK])
                for j in range(4)
            ]
            packed(32 * b + 16 * q, parts)
    kv = []
    for b in range(3):
        at = slice(b * BLOCK, (b + 1) * BLOCK)
        for part in ((dk_acc[at, :] * SCALE).astype(BF16), dv_acc[at, :].astype(BF16)):
            kv.append(dot(to_src[b], part))
    packed(64, kv[:4])
    packed(80, kv[4:])


def return_kernel(me_ref, place_ref, in_ref, dq_ref, dk_ref, dv_ref, u1, uk, uv):
    @pl.when(pl.program_id(0) == 0)
    def _():
        pair, half, rank = token_codes(place_ref, me_ref[0])

        def column(code):
            return spread(code)[1].astype(jnp.int32)

        first, second, halo = [column(c) for c in row_codes(pair, half, rank, 16)]
        second8 = column(row_codes(pair, half, rank, 8)[1])
        for at in range(2):
            lanes = iota((128, 128), 1) + 128 * at
            for j in range(4):
                rows = slice(j * 128, (j + 1) * 128)
                u1[rows, at * 128 : (at + 1) * 128] = onehot(lanes, first + 4 * j)
                u1[rows, 256 + at * 128 : 256 + (at + 1) * 128] = onehot(lanes, second + 4 * j)
            for j, u in enumerate((uk, uv)):
                u[:, at * 128 : (at + 1) * 128] = onehot(lanes, halo + 4 * j) + onehot(
                    lanes, first + 8 + 4 * j
                )
        for j, u in enumerate((uk, uv)):
            u[:, 256:384] = onehot(iota((128, 128), 1), second8 + 4 * j)

    def flat(start, rows):
        return in_ref[:, 0, start : start + rows, :].reshape(PAIRS * rows, 128)

    both = jnp.concatenate(
        [jnp.concatenate([flat(32 * b + 16 * q, 16) for q in range(2)], axis=1) for b in range(2)],
        axis=0,
    )
    moved = dot(u1[...], both).astype(BF16)
    for j in range(4):
        dq_ref[:, j * 256 : (j + 1) * 256] = moved[j * 128 : (j + 1) * 128, :]
    kv = jnp.concatenate([flat(64, 16), flat(80, 8)], axis=0)
    dk_ref[...] = dot(uk[...], kv).astype(BF16)
    dv_ref[...] = dot(uv[...], kv).astype(BF16)


def shards(query, key, value, grad_out, advantage, place, segment):
    me = (lax.axis_index("ctx") * 4 + lax.axis_index("head")).astype(jnp.int32).reshape(1)
    place2 = place.reshape(128, 128)
    doc2 = segment.reshape(128, 128)
    smem = pl.BlockSpec(memory_space=pltpu.SMEM)
    vmem = pl.BlockSpec(memory_space=pltpu.VMEM)
    whole = pl.BlockSpec((128, 128), lambda g: (0, 0))
    params = pltpu.CompilerParams(vmem_limit_bytes=VMEM_LIMIT)

    sent = pl.pallas_call(
        send_kernel,
        grid=(GROUPS,),
        in_specs=[
            smem,
            whole,
            pl.BlockSpec((1, 128), lambda g: (0, 0)),
            pl.BlockSpec((128, WIDTH * D), lambda g: (0, g)),
            pl.BlockSpec((128, D), lambda g: (0, g)),
            pl.BlockSpec((128, D), lambda g: (0, g)),
            pl.BlockSpec((128, WIDTH * D), lambda g: (0, g)),
        ],
        out_specs=pl.BlockSpec((PAIRS, 1, SEND_ROWS, 128), lambda g: (0, g, 0, 0)),
        out_shape=jax.ShapeDtypeStruct((PAIRS, GROUPS, SEND_ROWS, 128), BF16),
        scratch_shapes=[
            pltpu.VMEM((256, 512), BF16),
            pltpu.VMEM((256, 512), BF16),
            pltpu.VMEM((256, 512), BF16),
            pltpu.VMEM((128, 256), BF16),
            pltpu.VMEM((128, 128), F32),
        ],
        compiler_params=params,
        name="to_blocks",
    )(me, place2, advantage.reshape(1, 128), query, key, value, grad_out)

    arrived = lax.all_to_all(
        sent.reshape(128, SEND_ROWS, 128), ("ctx", "head"), split_axis=0, concat_axis=0, tiled=True
    )

    gradients = pl.pallas_call(
        attend_kernel,
        in_specs=[smem, smem, vmem, vmem, vmem],
        out_specs=vmem,
        out_shape=jax.ShapeDtypeStruct((128, BACK_ROWS, 128), BF16),
        scratch_shapes=[
            pltpu.VMEM((3, BLOCK, BLOCK), BF16),
            pltpu.VMEM((3, BLOCK, BLOCK), BF16),
            pltpu.VMEM((2048, 128), F32),
            pltpu.VMEM((WIDTH, 2 * BLOCK, D), BF16),
            pltpu.VMEM((WIDTH, 2 * BLOCK, D), BF16),
            pltpu.VMEM((3 * BLOCK, D), BF16),
            pltpu.VMEM((3 * BLOCK, D), BF16),
            pltpu.VMEM((D, 3 * BLOCK), BF16),
            pltpu.VMEM((12, 128, 128), F32),
            pltpu.VMEM((5, WIDTH, 128, 128), F32),
            pltpu.VMEM((5, WIDTH, 128, 128), F32),
            pltpu.VMEM((D, WIDTH * 128), F32),
            pltpu.VMEM((WIDTH, D, 2 * BLOCK), BF16),
            pltpu.VMEM((3 * BLOCK, D), F32),
            pltpu.VMEM((3 * BLOCK, D), F32),
        ],
        compiler_params=params,
        name="attend",
    )(me, segment, place2, doc2, arrived)

    back = lax.all_to_all(gradients, ("ctx", "head"), split_axis=0, concat_axis=0, tiled=True)

    return pl.pallas_call(
        return_kernel,
        grid=(GROUPS,),
        in_specs=[
            smem,
            whole,
            pl.BlockSpec((PAIRS, 1, BACK_ROWS, 128), lambda g: (0, g, 0, 0)),
        ],
        out_specs=[
            pl.BlockSpec((128, WIDTH * D), lambda g: (0, g)),
            pl.BlockSpec((128, D), lambda g: (0, g)),
            pl.BlockSpec((128, D), lambda g: (0, g)),
        ],
        out_shape=[
            jax.ShapeDtypeStruct((128, GROUPS * WIDTH * D), BF16),
            jax.ShapeDtypeStruct((128, GROUPS * D), BF16),
            jax.ShapeDtypeStruct((128, GROUPS * D), BF16),
        ],
        scratch_shapes=[
            pltpu.VMEM((512, 512), BF16),
            pltpu.VMEM((128, 384), BF16),
            pltpu.VMEM((128, 384), BF16),
        ],
        compiler_params=params,
        name="to_rows",
    )(me, place2, back.reshape(PAIRS, GROUPS, BACK_ROWS, 128))


def solution(mesh):
    spec = P(("ctx", "head"), None)
    in_specs = (spec, spec, spec, spec, P(("ctx", "head")), P(), P())
    return jax.shard_map(
        shards, mesh=mesh, in_specs=in_specs, out_specs=(spec, spec, spec), check_vma=False
    )
```

```python
import functools

import jax
import jax.numpy as jnp
from jax import lax
from jax.experimental import pallas as pl
from jax.experimental.pallas import tpu as pltpu
from jax.sharding import PartitionSpec as P

GROUPS = 8
WIDTH = 8
D = 128
BLOCK = 512
PAIRS = 16
SPAN = 3 * BLOCK
SCALE = D ** (-0.5)
LOG2E = 1.4426950408889634
NEG = -1e30
F32 = jnp.float32
BF16 = jnp.bfloat16

SEND_ROWS = 8 * (2 * WIDTH + 3)
BACK_ROWS = 8 * (WIDTH + 3)
VMEM_LIMIT = 56 * 1024 * 1024
PER = 8
QB = 1
IN_ORDER = (4, 0, 1, 2, 3)


def iota(shape, dim):
    return lax.broadcasted_iota(jnp.int32, shape, dim)


def dot(a, b):
    return jnp.dot(a, b, preferred_element_type=F32)


def dot_nt(a, b):
    return lax.dot_general(a, b, (((1,), (1,)), ((), ())), preferred_element_type=F32)


def onehot(index, code):
    return (index == code).astype(F32).astype(BF16)


def token_codes(place_ref, me):
    row = place_ref[pl.ds(me, 1), :]
    dest = lax.shift_right_logical(row, 9)
    across = jnp.broadcast_to(dest.astype(F32), (128, 128))
    before = (across == jnp.transpose(across)) & (iota((128, 128), 0) < iota((128, 128), 1))
    rank = jnp.sum(before.astype(F32), axis=0, keepdims=True).astype(jnp.int32)
    pair, half, odd = lax.shift_right_logical(dest, 1), dest & 1, me & 1
    own = pair * 8 + (half ^ odd) * 4 + rank
    later = (half == 1) & (pair < PAIRS - 1)
    halo_key = jnp.where(later, pair * 8 + 8 + odd * 4 + rank, -1)
    halo_value = jnp.where(later, pair * 8 + 8 + (1 - odd) * 4 + rank, -1)
    return own, halo_key, halo_value


def tiles_to(out_ref, start, tiles):
    n = out_ref.shape[0]
    for i in range(0, len(tiles), 2):
        part = [t.reshape(n, 8, 128) for t in tiles[i : i + 2]]
        part = jnp.concatenate(part, axis=1) if len(part) == 2 else part[0]
        at = start + 8 * i
        out_ref[:, at : at + part.shape[1], :] = part.astype(BF16)


def send_kernel(me_ref, place_ref, adv_ref, q_ref, g_ref, k_ref, v_ref, out_ref, own, halo_k, halo_v, adv):
    @pl.when(pl.program_id(0) == 0)
    def _():
        for ref, code in zip((own, halo_k, halo_v), token_codes(place_ref, me_ref[0])):
            ref[...] = onehot(iota((128, 128), 0), code)
        adv[...] = jnp.transpose(jnp.broadcast_to(adv_ref[...], (128, 128)))

    weight, move = adv[...], own[...]
    grad = jnp.concatenate(
        [(g_ref[:, h * D : (h + 1) * D].astype(F32) * weight).astype(BF16) for h in range(WIDTH)], axis=1
    )
    tiles = []
    for block in (q_ref[...], grad):
        moved = dot(move, block)
        tiles += [moved[:, h * D : (h + 1) * D] for h in range(WIDTH)]
    tiles += [dot(move, k_ref[...]), dot(move, v_ref[...])]
    tiles += [dot(halo_k[...], k_ref[...]) + dot(halo_v[...], v_ref[...])]
    tiles_to(out_ref.at[:, 0], 0, tiles)


def source_maps(place, block, spread_ref, gather_ref, column):
    own = lax.shift_right_logical(place, 9) == block
    member = own.astype(F32)
    earlier = onehot(jnp.int32(1), (iota((128, 128), 0) < iota((128, 128), 1)).astype(jnp.int32))
    rank = dot(member.astype(BF16), earlier)
    picked = jnp.where(own, (place - block * BLOCK + 1).astype(F32), 0.0)
    for r in range(4):
        part = jnp.sum(jnp.where(rank == r, picked, 0.0), axis=1, keepdims=True) - 1.0
        column[pl.ds(r, 128, stride=4), :] = jnp.broadcast_to(part, (128, 128))
    for b in range(4):
        at = slice(b * 128, (b + 1) * 128)
        whole = column[at, :]
        gather_ref[at, :] = jnp.concatenate(
            [onehot(iota((128, 128), 1) + 128 * c, whole.astype(jnp.int32)) for c in range(4)], axis=1
        )
        row = jnp.transpose(whole)[0:1, :].astype(jnp.int32)
        spread_ref[:, at] = onehot(iota((BLOCK, 128), 0), row)


def attend_kernel(
    me_ref, place_ref, doc_ref, in_hbm, out_hbm,
    in_ref, out_ref, to_pos, to_src, column, arrived, qs, ws, ks, vs, kt, doc_t, dq_t, dk_acc, dv_acc, counts,
    in_sem, out_sem,
):
    def copy_in(i):
        at = pl.ds(32 * i, 32 if i < 4 else 24)
        return pltpu.make_async_copy(in_hbm.at[:, at], in_ref.at[:, at], in_sem.at[i])

    for i in IN_ORDER:
        copy_in(i).start()

    pair = lax.shift_right_logical(me_ref[0], 3)
    place = place_ref[...]
    even = (iota((128, 128), 0) & 1) == 0
    place_f = place.astype(F32)
    swapped = jnp.where(even, pltpu.roll(place_f, 127, 0), pltpu.roll(place_f, 1, 0)).astype(jnp.int32)
    for i, (rows, block) in enumerate(
        ((place, 2 * pair), (swapped, 2 * pair + 1), (place, 2 * pair - 1), (swapped, 2 * pair - 1))
    ):
        source_maps(rows, block, to_pos.at[i], to_src.at[i], column.at[i])

    docs = doc_ref[...]
    block_at = iota((128, 128), 0)
    last = iota((128, 128), 1) == 127
    for ib in range(8):
        block = 8 * pair + ib
        first_doc = doc_ref[pl.ds(block, 1), :][:, 0:1]
        near = last & (block_at < block) & (block_at >= block - 4) & (docs >= first_doc)
        counts[ib] = 1 + jnp.sum(near.astype(F32)).astype(jnp.int32)
    for b in range(12):
        at = 8 * pair - 4 + b
        doc = doc_ref[pl.ds(jnp.maximum(at, 0), 1), :].astype(F32)
        doc = jnp.where(at >= 0, doc, -2.0)
        doc_t[b * 128 : (b + 1) * 128, :] = jnp.transpose(jnp.broadcast_to(doc, (128, 128)))
    dk_acc[...] = jnp.zeros_like(dk_acc)
    dv_acc[...] = jnp.zeros_like(dv_acc)

    upper = iota((64, 8, 128), 1) < 4

    def halves(tile):
        rows = in_ref[:, 8 * tile : 8 * tile + 8, :].astype(F32).reshape(64, 16, 128)
        a, b = rows[:, :8], rows[:, 8:]
        return (
            jnp.where(upper, a, b).reshape(BLOCK, 128).astype(BF16),
            jnp.where(upper, b, a).reshape(BLOCK, 128).astype(BF16),
        )

    def placed(t, count, half, map_at):
        both = jnp.concatenate([arrived[t + i, half] for i in range(count)], axis=1)
        return dot(to_pos[map_at], both).astype(BF16)

    for i in IN_ORDER:
        copy_in(i).wait()
        tiles = range(4 * i, min(4 * i + 4, 19))
        for t in tiles:
            arrived[t, 0], arrived[t, 1] = halves(t)
        if i < 4:
            target, first = (qs, 4 * i) if i < 2 else (ws, 4 * i - 8)
            for h in range(0, 4, 2):
                for b in range(2):
                    moved = placed(4 * i + h, 2, b, b)
                    at = slice(b * BLOCK, (b + 1) * BLOCK)
                    target[first + h, at, :] = moved[:, :128]
                    target[first + h + 1, at, :] = moved[:, 128:]
        else:
            for b in range(2):
                moved = placed(16, 2, b, b)
                at = slice((b + 1) * BLOCK, (b + 2) * BLOCK)
                ks[at, :] = moved[:, :128]
                vs[at, :] = moved[:, 128:]
            ks[:BLOCK, :] = placed(18, 1, 0, 2)
            vs[:BLOCK, :] = placed(18, 1, 1, 3)
            kt[...] = dot_nt(onehot(iota((128, 128), 0), iota((128, 128), 1)), ks[...]).astype(BF16)

    def over(first, n):
        length = n * 128
        for ib in [first + k for k in range(QB)]:
            rows = pl.ds(pl.multiple_of(ib * 128, 128), 128)
            query_doc = doc_ref[pl.ds(8 * pair + ib, 1), :].astype(F32)
            window = pl.ds(pl.multiple_of((ib + 5 - n) * 128, 128), length)
            keys, values, keys_t = ks[window, :], vs[window, :], kt[:, window]
            later = iota((length, 128), 0) - iota((length, 128), 1) > length - 128
            bias = jnp.where((doc_t[window, :] == query_doc) & ~later, 0.0, NEG)
            bias = jnp.concatenate([bias] * PER, axis=1)
            all_weights, all_dscore, all_query, all_grad = [], [], [], []
            for h in range(0, WIDTH, PER):
                query = jnp.concatenate([qs[h + k, rows, :] for k in range(PER)], axis=0)
                grad = jnp.concatenate([ws[h + k, rows, :] for k in range(PER)], axis=0)
                score = dot_nt(keys, query) * (SCALE * LOG2E) + bias
                prob = jnp.exp2(score - jnp.max(score, axis=0, keepdims=True))
                prob = prob * (1.0 / jnp.sum(prob, axis=0, keepdims=True))
                weights = prob.astype(BF16)
                dprob = dot_nt(values, grad)
                delta = jnp.sum(weights.astype(F32) * dprob, axis=0, keepdims=True)
                dscore = (prob * SCALE * (dprob - delta)).astype(BF16)
                dq = dot(keys_t, dscore).astype(BF16)
                for k in range(PER):
                    dq_t[h + k, :, rows] = dq[:, k * 128 : (k + 1) * 128]
                all_weights.append(weights)
                all_dscore.append(dscore)
                all_query.append(query)
                all_grad.append(grad)
            dv_acc[window, :] += dot(
                jnp.concatenate(all_weights, axis=1), jnp.concatenate(all_grad, axis=0)
            )
            dk_acc[window, :] += dot(
                jnp.concatenate(all_dscore, axis=1), jnp.concatenate(all_query, axis=0)
            )

    def query_blocks(i, carry):
        first = i * QB
        count = counts[first]
        for k in range(1, QB):
            count = jnp.maximum(count, counts[first + k])
        pl.when(count <= 2)(lambda: over(first, 2))
        pl.when(count == 3)(lambda: over(first, 3))
        pl.when(count >= 4)(lambda: over(first, 5))
        return carry

    lax.fori_loop(0, 8 // QB, query_blocks, 0)

    def woven(one, two):
        a, b = one.reshape(64, 8, 128), two.reshape(64, 8, 128)
        rows = jnp.concatenate([jnp.where(upper, a, b), jnp.where(upper, b, a)], axis=1)
        return rows.reshape(1024, 128)

    def copy_out(i):
        at = pl.ds(16 * i, 16 if i < 4 else 24)
        return pltpu.make_async_copy(out_ref.at[:, at], out_hbm.at[:, at], out_sem.at[i])

    def rounded(b):
        at = slice(b * BLOCK, (b + 1) * BLOCK)
        return dk_acc[at, :].astype(BF16), dv_acc[at, :].astype(BF16)

    both = [dot(to_src[b], jnp.concatenate(rounded(b + 1), axis=1)) for b in range(2)]
    halo_key, halo_value = rounded(0)
    tiles = [woven(both[0][:, i * 128 : (i + 1) * 128], both[1][:, i * 128 : (i + 1) * 128]) for i in range(2)]
    tiles.append(woven(dot(to_src[2], halo_key), dot(to_src[3], halo_value)))
    tiles_to(out_ref, 8 * WIDTH, tiles)
    copy_out(4).start()
    for h in range(0, WIDTH, 2):
        both = [
            dot_nt(
                to_src[b],
                jnp.concatenate([dq_t[h + i, :, b * BLOCK : (b + 1) * BLOCK] for i in range(2)], axis=0),
            )
            for b in range(2)
        ]
        tiles = [woven(both[0][:, i * 128 : (i + 1) * 128], both[1][:, i * 128 : (i + 1) * 128]) for i in range(2)]
        tiles_to(out_ref, 8 * h, tiles)
        copy_out(h // 2).start()
    for i in range(5):
        copy_out(i).wait()


def return_kernel(me_ref, place_ref, in_ref, dq_ref, dk_ref, dv_ref, own, keys, values):
    @pl.when(pl.program_id(0) == 0)
    def _():
        def column(code):
            return jnp.transpose(jnp.broadcast_to(code.astype(F32), (128, 128))).astype(jnp.int32)

        def wide(code, tile):
            spread = lax.shift_right_logical(code, 3) * 16 + (code & 7) + 8 * tile
            return jnp.where(code >= 0, spread, -1)

        own_c, key_c, value_c = [column(c) for c in token_codes(place_ref, me_ref[0])]
        for at in range(2):
            lanes = iota((128, 128), 1) + 128 * at
            cols = slice(at * 128, (at + 1) * 128)
            for i in range(2):
                own[i * 128 : (i + 1) * 128, cols] = onehot(lanes, wide(own_c, i))
        keys[...] = onehot(iota((128, 128), 1), key_c)
        values[...] = onehot(iota((128, 128), 1), value_c)

    def pair_of(tile):
        return in_ref[:, 0, 8 * tile : 8 * tile + 16, :].reshape(256, 128)

    both = own[...]
    for h in range(0, WIDTH, 4):
        moved = dot(both, jnp.concatenate([pair_of(h), pair_of(h + 2)], axis=1)).astype(BF16)
        for i, (a, b) in enumerate(((0, 0), (1, 0), (0, 1), (1, 1))):
            dq_ref[:, (h + i) * D : (h + i + 1) * D] = moved[a * 128 : (a + 1) * 128, b * 128 : (b + 1) * 128]
    moved = dot(both, pair_of(WIDTH))
    halo = in_ref[:, 0, 8 * WIDTH + 16 :, :].astype(F32).reshape(128, 128).astype(BF16)
    dk_ref[...] = (moved[:128] + dot(keys[...], halo)).astype(BF16)
    dv_ref[...] = (moved[128:] + dot(values[...], halo)).astype(BF16)


SMEM = pl.BlockSpec(memory_space=pltpu.SMEM)
VMEM = pl.BlockSpec(memory_space=pltpu.VMEM)
ANY = pl.BlockSpec(memory_space=pl.ANY)
WHOLE = pl.BlockSpec((128, 128), lambda g: (0, 0))


def params():
    return pltpu.CompilerParams(vmem_limit_bytes=VMEM_LIMIT)


def exchanged(rows):
    return lax.all_to_all(rows, ("ctx", "head"), split_axis=0, concat_axis=0, tiled=True)


def sent(me, place2, advantage, query, grad_out, key, value):
    wide = pl.BlockSpec((128, WIDTH * D), lambda g: (0, g))
    narrow = pl.BlockSpec((128, D), lambda g: (0, g))
    square = pltpu.VMEM((128, 128), BF16)
    out = pl.pallas_call(
        send_kernel,
        grid=(GROUPS,),
        in_specs=[SMEM, WHOLE, pl.BlockSpec((1, 128), lambda g: (0, 0)), wide, wide, narrow, narrow],
        out_specs=pl.BlockSpec((PAIRS, 1, SEND_ROWS, 128), lambda g: (0, g, 0, 0)),
        out_shape=jax.ShapeDtypeStruct((PAIRS, GROUPS, SEND_ROWS, 128), BF16),
        scratch_shapes=[square, square, square, pltpu.VMEM((128, 128), F32)],
        compiler_params=params(),
        name="to_blocks",
    )(me, place2, advantage.reshape(1, 128), query, grad_out, key, value)
    return out.reshape(PAIRS * GROUPS, SEND_ROWS, 128)


def shards(query, key, value, grad_out, advantage, place, segment):
    me = (lax.axis_index("ctx") * 4 + lax.axis_index("head")).astype(jnp.int32).reshape(1)
    place2 = place.reshape(128, 128)
    doc2 = segment.reshape(128, 128)
    arrived = exchanged(sent(me, place2, advantage, query, grad_out, key, value))

    maps = pltpu.VMEM((4, BLOCK, BLOCK), BF16)
    heads = pltpu.VMEM((WIDTH, 2 * BLOCK, D), BF16)
    gradients = pl.pallas_call(
        attend_kernel,
        in_specs=[SMEM, VMEM, VMEM, ANY],
        out_specs=ANY,
        out_shape=jax.ShapeDtypeStruct((128, BACK_ROWS, 128), BF16),
        scratch_shapes=[
            pltpu.VMEM((128, SEND_ROWS, 128), BF16),
            pltpu.VMEM((128, BACK_ROWS, 128), BF16),
            maps,
            maps,
            pltpu.VMEM((4, BLOCK, 128), F32),
            pltpu.VMEM((19, 2, BLOCK, 128), BF16),
            heads,
            heads,
            pltpu.VMEM((SPAN, D), BF16),
            pltpu.VMEM((SPAN, D), BF16),
            pltpu.VMEM((D, SPAN), BF16),
            pltpu.VMEM((SPAN, 128), F32),
            pltpu.VMEM((WIDTH, D, 2 * BLOCK), BF16),
            pltpu.VMEM((SPAN, D), F32),
            pltpu.VMEM((SPAN, D), F32),
            pltpu.SMEM((8,), jnp.int32),
            pltpu.SemaphoreType.DMA((5,)),
            pltpu.SemaphoreType.DMA((5,)),
        ],
        compiler_params=params(),
        name="attend",
    )(me, place2, doc2, arrived)

    back = exchanged(gradients)
    rows = BACK_ROWS
    return pl.pallas_call(
        return_kernel,
        grid=(GROUPS,),
        in_specs=[SMEM, WHOLE, pl.BlockSpec((PAIRS, 1, rows, 128), lambda g: (0, g, 0, 0))],
        out_specs=[
            pl.BlockSpec((128, WIDTH * D), lambda g: (0, g)),
            pl.BlockSpec((128, D), lambda g: (0, g)),
            pl.BlockSpec((128, D), lambda g: (0, g)),
        ],
        out_shape=[
            jax.ShapeDtypeStruct((128, GROUPS * WIDTH * D), BF16),
            jax.ShapeDtypeStruct((128, GROUPS * D), BF16),
            jax.ShapeDtypeStruct((128, GROUPS * D), BF16),
        ],
        scratch_shapes=[
            pltpu.VMEM((256, 256), BF16),
            pltpu.VMEM((128, 128), BF16),
            pltpu.VMEM((128, 128), BF16),
        ],
        compiler_params=params(),
        name="to_rows",
    )(me, place2, back.reshape(PAIRS, GROUPS, rows, 128))


def solution(mesh):
    spec = P(("ctx", "head"), None)
    in_specs = (spec, spec, spec, spec, P(("ctx", "head")), P(), P())
    return jax.shard_map(
        shards, mesh=mesh, in_specs=in_specs, out_specs=(spec, spec, spec), check_vma=False
    )
```

```python
import jax
import jax.numpy as jnp
from jax import lax
from jax.experimental import pallas as pl
from jax.experimental.pallas import tpu as pltpu
from jax.sharding import PartitionSpec as P

GROUPS = 8
WIDTH = 8
D = 128
BLOCK = 512
PAIRS = 16
SPAN = 3 * BLOCK
SCALE = D ** (-0.5)
LOG2E = 1.4426950408889634
NEG = -1e30
F32 = jnp.float32
BF16 = jnp.bfloat16

SEND_ROWS = 8 * (2 * WIDTH + 3)
BACK_ROWS = 8 * (WIDTH + 3)
VMEM_LIMIT = 56 * 1024 * 1024
PER = 8
QB = 1
IN_ORDER = (4, 0, 1, 2, 3)


def iota(shape, dim):
    return lax.broadcasted_iota(jnp.int32, shape, dim)


def dot(a, b):
    return jnp.dot(a, b, preferred_element_type=F32)


def dot_nt(a, b):
    return lax.dot_general(a, b, (((1,), (1,)), ((), ())), preferred_element_type=F32)


def onehot(index, code):
    return (index == code).astype(F32).astype(BF16)


def token_codes(place_ref, me):
    row = place_ref[pl.ds(me & 7, 1), :]
    dest = lax.shift_right_logical(row, 9)
    across = jnp.broadcast_to(dest.astype(F32), (128, 128))
    before = (across == jnp.transpose(across)) & (iota((128, 128), 0) < iota((128, 128), 1))
    rank = jnp.sum(before.astype(F32), axis=0, keepdims=True).astype(jnp.int32)
    pair, half, odd = lax.shift_right_logical(dest, 1), dest & 1, me & 1
    own = pair * 8 + (half ^ odd) * 4 + rank
    later = (half == 1) & (pair < PAIRS - 1)
    halo_key = jnp.where(later, pair * 8 + 8 + odd * 4 + rank, -1)
    halo_value = jnp.where(later, pair * 8 + 8 + (1 - odd) * 4 + rank, -1)
    return own, halo_key, halo_value


def tiles_to(out_ref, start, tiles):
    n = out_ref.shape[0]
    for i in range(0, len(tiles), 2):
        part = [t.reshape(n, 8, 128) for t in tiles[i : i + 2]]
        part = jnp.concatenate(part, axis=1) if len(part) == 2 else part[0]
        at = start + 8 * i
        out_ref[:, at : at + part.shape[1], :] = part.astype(BF16)


def fetch_place(place_hbm, place_ref, me, sem):
    first = pl.multiple_of(lax.shift_right_logical(me, 3) * 8, 8)
    copy = pltpu.make_async_copy(place_hbm.at[pl.ds(first, 8), :], place_ref, sem)
    copy.start()
    return copy


def send_kernel(
    me_ref, place_hbm, adv_hbm, q_hbm, g_hbm, k_hbm, v_hbm, out_hbm,
    place_ref, adv_ref, q_ref, g_ref, k_ref, v_ref, out_ref, sems, small,
):
    place_copy = fetch_place(place_hbm, place_ref, me_ref[0], small.at[0])
    adv_copy = pltpu.make_async_copy(adv_hbm, adv_ref, small.at[1])
    adv_copy.start()
    pairs = ((q_hbm, q_ref), (g_hbm, g_ref), (k_hbm, k_ref), (v_hbm, v_ref))

    def copies_in(g):
        for i, (source, into) in enumerate(pairs):
            width = WIDTH * D if i < 2 else D
            at = slice(g * width, (g + 1) * width)
            yield pltpu.make_async_copy(source.at[:, at], into.at[:, at], sems.at[i, g])

    def copy_out(g):
        return pltpu.make_async_copy(out_ref.at[:, g], out_hbm.at[:, g], sems.at[4, g])

    for g in range(GROUPS):
        for copy in copies_in(g):
            copy.start()
    place_copy.wait()
    adv_copy.wait()
    rows = iota((128, 128), 0)
    own, halo_k, halo_v = [onehot(rows, code) for code in token_codes(place_ref, me_ref[0])]
    weight = jnp.transpose(jnp.broadcast_to(adv_ref[...], (128, 128)))
    for g in range(GROUPS):
        for copy in copies_in(g):
            copy.wait()
        wide = slice(g * WIDTH * D, (g + 1) * WIDTH * D)
        narrow = slice(g * D, (g + 1) * D)
        grad = g_ref[:, wide]
        grad = jnp.concatenate(
            [(grad[:, h * D : (h + 1) * D].astype(F32) * weight).astype(BF16) for h in range(WIDTH)], axis=1
        )
        tiles = []
        for block in (q_ref[:, wide], grad):
            moved = dot(own, block)
            tiles += [moved[:, h * D : (h + 1) * D] for h in range(WIDTH)]
        key, value = k_ref[:, narrow], v_ref[:, narrow]
        tiles += [dot(own, key), dot(own, value), dot(halo_k, key) + dot(halo_v, value)]
        tiles_to(out_ref.at[:, g], 0, tiles)
        copy_out(g).start()
    for g in range(GROUPS):
        copy_out(g).wait()


def source_maps(place, block, spread_ref, gather_ref, column):
    own = lax.shift_right_logical(place, 9) == block
    member = own.astype(F32)
    earlier = onehot(jnp.int32(1), (iota((128, 128), 0) < iota((128, 128), 1)).astype(jnp.int32))
    rank = dot(member.astype(BF16), earlier)
    picked = jnp.where(own, (place - block * BLOCK + 1).astype(F32), 0.0)
    for r in range(4):
        part = jnp.sum(jnp.where(rank == r, picked, 0.0), axis=1, keepdims=True) - 1.0
        column[pl.ds(r, 128, stride=4), :] = jnp.broadcast_to(part, (128, 128))
    for b in range(4):
        at = slice(b * 128, (b + 1) * 128)
        whole = column[at, :]
        gather_ref[at, :] = jnp.concatenate(
            [onehot(iota((128, 128), 1) + 128 * c, whole.astype(jnp.int32)) for c in range(4)], axis=1
        )
        row = jnp.transpose(whole)[0:1, :].astype(jnp.int32)
        spread_ref[:, at] = onehot(iota((BLOCK, 128), 0), row)


def attend_kernel(
    me_ref, place_hbm, doc_hbm, in_hbm, out_hbm,
    place_ref, doc_ref, in_ref, out_ref, to_pos, to_src, column, arrived, qs, ws, ks, vs, kt, doc_t, dq_t, dk_acc, dv_acc, counts,
    in_sem, out_sem, small,
):
    def copy_in(i):
        at = pl.ds(32 * i, 32 if i < 4 else 24)
        return pltpu.make_async_copy(in_hbm.at[:, at], in_ref.at[:, at], in_sem.at[i])

    tables = [
        pltpu.make_async_copy(place_hbm, place_ref, small.at[0]),
        pltpu.make_async_copy(doc_hbm, doc_ref, small.at[1]),
    ]
    for copy in tables:
        copy.start()
    for i in IN_ORDER:
        copy_in(i).start()
    for copy in tables:
        copy.wait()

    pair = lax.shift_right_logical(me_ref[0], 3)
    place = place_ref[...]
    even = (iota((128, 128), 0) & 1) == 0
    place_f = place.astype(F32)
    swapped = jnp.where(even, pltpu.roll(place_f, 127, 0), pltpu.roll(place_f, 1, 0)).astype(jnp.int32)
    for i, (rows, block) in enumerate(
        ((place, 2 * pair), (swapped, 2 * pair + 1), (place, 2 * pair - 1), (swapped, 2 * pair - 1))
    ):
        source_maps(rows, block, to_pos.at[i], to_src.at[i], column.at[i])

    docs = doc_ref[...]
    block_at = iota((128, 128), 0)
    last = iota((128, 128), 1) == 127
    for ib in range(8):
        block = 8 * pair + ib
        first_doc = doc_ref[pl.ds(block, 1), :][:, 0:1]
        near = last & (block_at < block) & (block_at >= block - 4) & (docs >= first_doc)
        counts[ib] = 1 + jnp.sum(near.astype(F32)).astype(jnp.int32)
    for b in range(12):
        at = 8 * pair - 4 + b
        doc = doc_ref[pl.ds(jnp.maximum(at, 0), 1), :].astype(F32)
        doc = jnp.where(at >= 0, doc, -2.0)
        doc_t[b * 128 : (b + 1) * 128, :] = jnp.transpose(jnp.broadcast_to(doc, (128, 128)))
    dk_acc[...] = jnp.zeros_like(dk_acc)
    dv_acc[...] = jnp.zeros_like(dv_acc)

    upper = iota((64, 8, 128), 1) < 4

    def halves(tile):
        rows = in_ref[:, 8 * tile : 8 * tile + 8, :].astype(F32).reshape(64, 16, 128)
        a, b = rows[:, :8], rows[:, 8:]
        return (
            jnp.where(upper, a, b).reshape(BLOCK, 128).astype(BF16),
            jnp.where(upper, b, a).reshape(BLOCK, 128).astype(BF16),
        )

    def placed(t, count, half, map_at):
        both = jnp.concatenate([arrived[t + i, half] for i in range(count)], axis=1)
        return dot(to_pos[map_at], both).astype(BF16)

    for i in IN_ORDER:
        copy_in(i).wait()
        tiles = range(4 * i, min(4 * i + 4, 19))
        for t in tiles:
            arrived[t, 0], arrived[t, 1] = halves(t)
        if i < 4:
            target, first = (qs, 4 * i) if i < 2 else (ws, 4 * i - 8)
            for h in range(0, 4, 2):
                for b in range(2):
                    moved = placed(4 * i + h, 2, b, b)
                    at = slice(b * BLOCK, (b + 1) * BLOCK)
                    target[first + h, at, :] = moved[:, :128]
                    target[first + h + 1, at, :] = moved[:, 128:]
        else:
            for b in range(2):
                moved = placed(16, 2, b, b)
                at = slice((b + 1) * BLOCK, (b + 2) * BLOCK)
                ks[at, :] = moved[:, :128]
                vs[at, :] = moved[:, 128:]
            ks[:BLOCK, :] = placed(18, 1, 0, 2)
            vs[:BLOCK, :] = placed(18, 1, 1, 3)
            kt[...] = dot_nt(onehot(iota((128, 128), 0), iota((128, 128), 1)), ks[...]).astype(BF16)

    def over(first, n):
        length = n * 128
        for ib in [first + k for k in range(QB)]:
            rows = pl.ds(pl.multiple_of(ib * 128, 128), 128)
            query_doc = doc_ref[pl.ds(8 * pair + ib, 1), :].astype(F32)
            window = pl.ds(pl.multiple_of((ib + 5 - n) * 128, 128), length)
            keys, values, keys_t = ks[window, :], vs[window, :], kt[:, window]
            later = iota((length, 128), 0) - iota((length, 128), 1) > length - 128
            bias = jnp.where((doc_t[window, :] == query_doc) & ~later, 0.0, NEG)
            bias = jnp.concatenate([bias] * PER, axis=1)
            all_weights, all_dscore, all_query, all_grad = [], [], [], []
            for h in range(0, WIDTH, PER):
                query = jnp.concatenate([qs[h + k, rows, :] for k in range(PER)], axis=0)
                grad = jnp.concatenate([ws[h + k, rows, :] for k in range(PER)], axis=0)
                score = dot_nt(keys, query) * (SCALE * LOG2E) + bias
                prob = jnp.exp2(score - jnp.max(score, axis=0, keepdims=True))
                prob = prob * (1.0 / jnp.sum(prob, axis=0, keepdims=True))
                weights = prob.astype(BF16)
                dprob = dot_nt(values, grad)
                delta = jnp.sum(weights.astype(F32) * dprob, axis=0, keepdims=True)
                dscore = (prob * SCALE * (dprob - delta)).astype(BF16)
                dq = dot(keys_t, dscore).astype(BF16)
                for k in range(PER):
                    dq_t[h + k, :, rows] = dq[:, k * 128 : (k + 1) * 128]
                all_weights.append(weights)
                all_dscore.append(dscore)
                all_query.append(query)
                all_grad.append(grad)
            dv_acc[window, :] += dot(
                jnp.concatenate(all_weights, axis=1), jnp.concatenate(all_grad, axis=0)
            )
            dk_acc[window, :] += dot(
                jnp.concatenate(all_dscore, axis=1), jnp.concatenate(all_query, axis=0)
            )

    def query_blocks(i, carry):
        first = i * QB
        count = counts[first]
        for k in range(1, QB):
            count = jnp.maximum(count, counts[first + k])
        pl.when(count <= 2)(lambda: over(first, 2))
        pl.when(count == 3)(lambda: over(first, 3))
        pl.when(count >= 4)(lambda: over(first, 5))
        return carry

    lax.fori_loop(0, 8 // QB, query_blocks, 0)

    def woven(one, two):
        a, b = one.reshape(64, 8, 128), two.reshape(64, 8, 128)
        rows = jnp.concatenate([jnp.where(upper, a, b), jnp.where(upper, b, a)], axis=1)
        return rows.reshape(1024, 128)

    def copy_out(i):
        at = pl.ds(16 * i, 16 if i < 4 else 24)
        return pltpu.make_async_copy(out_ref.at[:, at], out_hbm.at[:, at], out_sem.at[i])

    def rounded(b):
        at = slice(b * BLOCK, (b + 1) * BLOCK)
        return dk_acc[at, :].astype(BF16), dv_acc[at, :].astype(BF16)

    both = [dot(to_src[b], jnp.concatenate(rounded(b + 1), axis=1)) for b in range(2)]
    halo_key, halo_value = rounded(0)
    tiles = [woven(both[0][:, i * 128 : (i + 1) * 128], both[1][:, i * 128 : (i + 1) * 128]) for i in range(2)]
    tiles.append(woven(dot(to_src[2], halo_key), dot(to_src[3], halo_value)))
    tiles_to(out_ref, 8 * WIDTH, tiles)
    copy_out(4).start()
    for h in range(0, WIDTH, 2):
        both = [
            dot_nt(
                to_src[b],
                jnp.concatenate([dq_t[h + i, :, b * BLOCK : (b + 1) * BLOCK] for i in range(2)], axis=0),
            )
            for b in range(2)
        ]
        tiles = [woven(both[0][:, i * 128 : (i + 1) * 128], both[1][:, i * 128 : (i + 1) * 128]) for i in range(2)]
        tiles_to(out_ref, 8 * h, tiles)
        copy_out(h // 2).start()
    for i in range(5):
        copy_out(i).wait()


def return_kernel(
    me_ref, place_hbm, in_hbm, dq_hbm, dk_hbm, dv_hbm, place_ref, in_ref, dq_ref, dk_ref, dv_ref, sems, small
):
    place_copy = fetch_place(place_hbm, place_ref, me_ref[0], small.at[0])

    def copy_in(g):
        return pltpu.make_async_copy(in_hbm.at[:, g], in_ref.at[:, g], sems.at[0, g])

    def copy_dq(g):
        at = slice(g * WIDTH * D, (g + 1) * WIDTH * D)
        return pltpu.make_async_copy(dq_ref.at[:, at], dq_hbm.at[:, at], sems.at[1, g])

    for g in range(GROUPS):
        copy_in(g).start()
    place_copy.wait()

    def column(code):
        return jnp.transpose(jnp.broadcast_to(code.astype(F32), (128, 128))).astype(jnp.int32)

    def wide(code, tile):
        return lax.shift_right_logical(code, 3) * 16 + (code & 7) + 8 * tile

    own_c, key_c, value_c = [column(c) for c in token_codes(place_ref, me_ref[0])]
    own = jnp.concatenate(
        [
            jnp.concatenate([onehot(iota((128, 128), 1) + 128 * at, wide(own_c, i)) for at in range(2)], axis=1)
            for i in range(2)
        ],
        axis=0,
    )
    keys, values = onehot(iota((128, 128), 1), key_c), onehot(iota((128, 128), 1), value_c)
    for g in range(GROUPS):
        copy_in(g).wait()

        def pair_of(tile):
            return in_ref[:, g, 8 * tile : 8 * tile + 16, :].reshape(256, 128)

        for h in range(0, WIDTH, 4):
            moved = dot(own, jnp.concatenate([pair_of(h), pair_of(h + 2)], axis=1)).astype(BF16)
            for i, (a, b) in enumerate(((0, 0), (1, 0), (0, 1), (1, 1))):
                at = (g * WIDTH + h + i) * D
                dq_ref[:, at : at + D] = moved[a * 128 : (a + 1) * 128, b * 128 : (b + 1) * 128]
        moved = dot(own, pair_of(WIDTH))
        halo = in_ref[:, g, 8 * WIDTH + 16 :, :].astype(F32).reshape(128, 128).astype(BF16)
        narrow = slice(g * D, (g + 1) * D)
        dk_ref[:, narrow] = (moved[:128] + dot(keys, halo)).astype(BF16)
        dv_ref[:, narrow] = (moved[128:] + dot(values, halo)).astype(BF16)
        copy_dq(g).start()
    last = [
        pltpu.make_async_copy(dk_ref, dk_hbm, small.at[1]),
        pltpu.make_async_copy(dv_ref, dv_hbm, small.at[2]),
    ]
    for copy in last:
        copy.start()
    for g in range(GROUPS):
        copy_dq(g).wait()
    for copy in last:
        copy.wait()


SMEM = pl.BlockSpec(memory_space=pltpu.SMEM)
ANY = pl.BlockSpec(memory_space=pl.ANY)


def params():
    return pltpu.CompilerParams(vmem_limit_bytes=VMEM_LIMIT)


def exchanged(rows):
    return lax.all_to_all(rows, ("ctx", "head"), split_axis=0, concat_axis=0, tiled=True)


def sent(me, place2, advantage, query, grad_out, key, value):
    out = pl.pallas_call(
        send_kernel,
        in_specs=[SMEM] + [ANY] * 6,
        out_specs=ANY,
        out_shape=jax.ShapeDtypeStruct((PAIRS, GROUPS, SEND_ROWS, 128), BF16),
        scratch_shapes=[
            pltpu.VMEM((8, 128), jnp.int32),
            pltpu.VMEM((1, 128), F32),
            pltpu.VMEM((128, GROUPS * WIDTH * D), BF16),
            pltpu.VMEM((128, GROUPS * WIDTH * D), BF16),
            pltpu.VMEM((128, GROUPS * D), BF16),
            pltpu.VMEM((128, GROUPS * D), BF16),
            pltpu.VMEM((PAIRS, GROUPS, SEND_ROWS, 128), BF16),
            pltpu.SemaphoreType.DMA((5, GROUPS)),
            pltpu.SemaphoreType.DMA((2,)),
        ],
        compiler_params=params(),
        name="to_blocks",
    )(me, place2, advantage.reshape(1, 128), query, grad_out, key, value)
    return out.reshape(PAIRS * GROUPS, SEND_ROWS, 128)


def shards(query, key, value, grad_out, advantage, place, segment):
    me = (lax.axis_index("ctx") * 4 + lax.axis_index("head")).astype(jnp.int32).reshape(1)
    place2 = place.reshape(128, 128)
    doc2 = segment.reshape(128, 128)
    arrived = exchanged(sent(me, place2, advantage, query, grad_out, key, value))

    maps = pltpu.VMEM((4, BLOCK, BLOCK), BF16)
    heads = pltpu.VMEM((WIDTH, 2 * BLOCK, D), BF16)
    gradients = pl.pallas_call(
        attend_kernel,
        in_specs=[SMEM, ANY, ANY, ANY],
        out_specs=ANY,
        out_shape=jax.ShapeDtypeStruct((128, BACK_ROWS, 128), BF16),
        scratch_shapes=[
            pltpu.VMEM((128, 128), jnp.int32),
            pltpu.VMEM((128, 128), jnp.int32),
            pltpu.VMEM((128, SEND_ROWS, 128), BF16),
            pltpu.VMEM((128, BACK_ROWS, 128), BF16),
            maps,
            maps,
            pltpu.VMEM((4, BLOCK, 128), F32),
            pltpu.VMEM((19, 2, BLOCK, 128), BF16),
            heads,
            heads,
            pltpu.VMEM((SPAN, D), BF16),
            pltpu.VMEM((SPAN, D), BF16),
            pltpu.VMEM((D, SPAN), BF16),
            pltpu.VMEM((SPAN, 128), F32),
            pltpu.VMEM((WIDTH, D, 2 * BLOCK), BF16),
            pltpu.VMEM((SPAN, D), F32),
            pltpu.VMEM((SPAN, D), F32),
            pltpu.SMEM((8,), jnp.int32),
            pltpu.SemaphoreType.DMA((5,)),
            pltpu.SemaphoreType.DMA((5,)),
            pltpu.SemaphoreType.DMA((2,)),
        ],
        compiler_params=params(),
        name="attend",
    )(me, place2, doc2, arrived)

    back = exchanged(gradients)
    rows = BACK_ROWS
    wide = (128, GROUPS * WIDTH * D)
    narrow = (128, GROUPS * D)
    return pl.pallas_call(
        return_kernel,
        in_specs=[SMEM, ANY, ANY],
        out_specs=[ANY] * 3,
        out_shape=[jax.ShapeDtypeStruct(x, BF16) for x in (wide, narrow, narrow)],
        scratch_shapes=[
            pltpu.VMEM((8, 128), jnp.int32),
            pltpu.VMEM((PAIRS, GROUPS, rows, 128), BF16),
            pltpu.VMEM(wide, BF16),
            pltpu.VMEM(narrow, BF16),
            pltpu.VMEM(narrow, BF16),
            pltpu.SemaphoreType.DMA((2, GROUPS)),
            pltpu.SemaphoreType.DMA((3,)),
        ],
        compiler_params=params(),
        name="to_rows",
    )(me, place2, back.reshape(PAIRS, GROUPS, rows, 128))


def solution(mesh):
    spec = P(("ctx", "head"), None)
    in_specs = (spec, spec, spec, spec, P(("ctx", "head")), P(), P())
    return jax.shard_map(
        shards, mesh=mesh, in_specs=in_specs, out_specs=(spec, spec, spec), check_vma=False
    )
```

```python
import jax
import jax.numpy as jnp
from jax import lax
from jax.experimental import pallas as pl
from jax.experimental.pallas import tpu as pltpu
from jax.sharding import PartitionSpec as P

GROUPS = 8
WIDTH = 8
D = 128
BLOCK = 512
PAIRS = 16
SPAN = 3 * BLOCK
SCALE = D ** (-0.5)
LOG2E = 1.4426950408889634
NEG = -1e30
F32 = jnp.float32
BF16 = jnp.bfloat16

SEND_ROWS = 8 * (2 * WIDTH + 3)
BACK_ROWS = 8 * (WIDTH + 3)
SEND_MIB, ATTEND_MIB, RETURN_MIB = 56, 38, 20
PER = 8
QB = 1
IN_ORDER = (4, 0, 1, 2, 3)


def iota(shape, dim):
    return lax.broadcasted_iota(jnp.int32, shape, dim)


def dot(a, b):
    return jnp.dot(a, b, preferred_element_type=F32)


def dot_nt(a, b):
    return lax.dot_general(a, b, (((1,), (1,)), ((), ())), preferred_element_type=F32)


def onehot(index, code):
    return (index == code).astype(F32).astype(BF16)


def token_codes(place_ref, me):
    row = place_ref[pl.ds(me & 7, 1), :]
    dest = lax.shift_right_logical(row, 9)
    across = jnp.broadcast_to(dest.astype(F32), (128, 128))
    before = (across == jnp.transpose(across)) & (iota((128, 128), 0) < iota((128, 128), 1))
    rank = jnp.sum(before.astype(F32), axis=0, keepdims=True).astype(jnp.int32)
    pair, half, odd = lax.shift_right_logical(dest, 1), dest & 1, me & 1
    own = pair * 8 + (half ^ odd) * 4 + rank
    later = (half == 1) & (pair < PAIRS - 1)
    halo_key = jnp.where(later, pair * 8 + 8 + odd * 4 + rank, -1)
    halo_value = jnp.where(later, pair * 8 + 8 + (1 - odd) * 4 + rank, -1)
    return own, halo_key, halo_value


def tiles_to(out_ref, start, tiles):
    n = out_ref.shape[0]
    for i in range(0, len(tiles), 2):
        part = [t.reshape(n, 8, 128) for t in tiles[i : i + 2]]
        part = jnp.concatenate(part, axis=1) if len(part) == 2 else part[0]
        at = start + 8 * i
        out_ref[:, at : at + part.shape[1], :] = part.astype(BF16)


def fetch_place(place_hbm, place_ref, me, sem):
    first = pl.multiple_of(lax.shift_right_logical(me, 3) * 8, 8)
    copy = pltpu.make_async_copy(place_hbm.at[pl.ds(first, 8), :], place_ref, sem)
    copy.start()
    return copy


def send_kernel(
    me_ref, place_hbm, adv_hbm, q_hbm, g_hbm, k_hbm, v_hbm, out_hbm,
    place_ref, adv_ref, q_ref, g_ref, k_ref, v_ref, out_ref, sems, small,
):
    place_copy = fetch_place(place_hbm, place_ref, me_ref[0], small.at[0])
    adv_copy = pltpu.make_async_copy(adv_hbm, adv_ref, small.at[1])
    adv_copy.start()
    whole = [
        pltpu.make_async_copy(k_hbm, k_ref, small.at[2]),
        pltpu.make_async_copy(v_hbm, v_ref, small.at[3]),
    ]

    def copies_in(g):
        at = slice(g * WIDTH * D, (g + 1) * WIDTH * D)
        return [
            pltpu.make_async_copy(source.at[:, at], into.at[:, at], sems.at[i, g])
            for i, (source, into) in enumerate(((q_hbm, q_ref), (g_hbm, g_ref)))
        ]

    def copy_out(g):
        return pltpu.make_async_copy(out_ref.at[:, g], out_hbm.at[:, g], sems.at[2, g])

    for g in range(GROUPS):
        for copy in copies_in(g) + (whole if g == 0 else []):
            copy.start()
    place_copy.wait()
    adv_copy.wait()
    rows = iota((128, 128), 0)
    own, halo_k, halo_v = [onehot(rows, code) for code in token_codes(place_ref, me_ref[0])]
    weight = jnp.transpose(jnp.broadcast_to(adv_ref[...], (128, 128)))
    for g in range(GROUPS):
        for copy in copies_in(g) + (whole if g == 0 else []):
            copy.wait()
        wide = slice(g * WIDTH * D, (g + 1) * WIDTH * D)
        narrow = slice(g * D, (g + 1) * D)
        grad = g_ref[:, wide]
        grad = jnp.concatenate(
            [(grad[:, h * D : (h + 1) * D].astype(F32) * weight).astype(BF16) for h in range(WIDTH)], axis=1
        )
        tiles = []
        for block in (q_ref[:, wide], grad):
            moved = dot(own, block)
            tiles += [moved[:, h * D : (h + 1) * D] for h in range(WIDTH)]
        key, value = k_ref[:, narrow], v_ref[:, narrow]
        tiles += [dot(own, key), dot(own, value), dot(halo_k, key) + dot(halo_v, value)]
        tiles_to(out_ref.at[:, g], 0, tiles)
        copy_out(g).start()
    for g in range(GROUPS):
        copy_out(g).wait()


def source_maps(place, block, spread_ref, gather_ref, column):
    own = lax.shift_right_logical(place, 9) == block
    member = own.astype(F32)
    earlier = onehot(jnp.int32(1), (iota((128, 128), 0) < iota((128, 128), 1)).astype(jnp.int32))
    rank = dot(member.astype(BF16), earlier)
    picked = jnp.where(own, (place - block * BLOCK + 1).astype(F32), 0.0)
    for r in range(4):
        part = jnp.sum(jnp.where(rank == r, picked, 0.0), axis=1, keepdims=True) - 1.0
        column[pl.ds(r, 128, stride=4), :] = jnp.broadcast_to(part, (128, 128))
    for b in range(4):
        at = slice(b * 128, (b + 1) * 128)
        whole = column[at, :]
        gather_ref[at, :] = jnp.concatenate(
            [onehot(iota((128, 128), 1) + 128 * c, whole.astype(jnp.int32)) for c in range(4)], axis=1
        )
        row = jnp.transpose(whole)[0:1, :].astype(jnp.int32)
        spread_ref[:, at] = onehot(iota((BLOCK, 128), 0), row)


def attend_kernel(
    me_ref, place_hbm, doc_hbm, in_ref, out_ref,
    place_ref, doc_ref, to_pos, to_src, column, arrived, qs, ws, ks, vs, kt, doc_t, dq_t, dk_acc, dv_acc, counts,
    small,
):
    tables = [
        pltpu.make_async_copy(place_hbm, place_ref, small.at[0]),
        pltpu.make_async_copy(doc_hbm, doc_ref, small.at[1]),
    ]
    for copy in tables:
        copy.start()
    for copy in tables:
        copy.wait()

    pair = lax.shift_right_logical(me_ref[0], 3)
    place = place_ref[...]
    even = (iota((128, 128), 0) & 1) == 0
    place_f = place.astype(F32)
    swapped = jnp.where(even, pltpu.roll(place_f, 127, 0), pltpu.roll(place_f, 1, 0)).astype(jnp.int32)
    for i, (rows, block) in enumerate(
        ((place, 2 * pair), (swapped, 2 * pair + 1), (place, 2 * pair - 1), (swapped, 2 * pair - 1))
    ):
        source_maps(rows, block, to_pos.at[i], to_src.at[i], column.at[i])

    docs = doc_ref[...]
    block_at = iota((128, 128), 0)
    last = iota((128, 128), 1) == 127
    for ib in range(8):
        block = 8 * pair + ib
        first_doc = doc_ref[pl.ds(block, 1), :][:, 0:1]
        near = last & (block_at < block) & (block_at >= block - 4) & (docs >= first_doc)
        counts[ib] = 1 + jnp.sum(near.astype(F32)).astype(jnp.int32)
    for b in range(12):
        at = 8 * pair - 4 + b
        doc = doc_ref[pl.ds(jnp.maximum(at, 0), 1), :].astype(F32)
        doc = jnp.where(at >= 0, doc, -2.0)
        doc_t[b * 128 : (b + 1) * 128, :] = jnp.transpose(jnp.broadcast_to(doc, (128, 128)))
    dk_acc[...] = jnp.zeros_like(dk_acc)
    dv_acc[...] = jnp.zeros_like(dv_acc)

    upper = iota((64, 8, 128), 1) < 4

    def halves(tile):
        rows = in_ref[:, 8 * tile : 8 * tile + 8, :].astype(F32).reshape(64, 16, 128)
        a, b = rows[:, :8], rows[:, 8:]
        return (
            jnp.where(upper, a, b).reshape(BLOCK, 128).astype(BF16),
            jnp.where(upper, b, a).reshape(BLOCK, 128).astype(BF16),
        )

    def placed(t, count, half, map_at):
        both = jnp.concatenate([arrived[t + i, half] for i in range(count)], axis=1)
        return dot(to_pos[map_at], both).astype(BF16)

    for i in IN_ORDER:
        tiles = range(4 * i, min(4 * i + 4, 19))
        for t in tiles:
            arrived[t, 0], arrived[t, 1] = halves(t)
        if i < 4:
            target, first = (qs, 4 * i) if i < 2 else (ws, 4 * i - 8)
            for h in range(0, 4, 2):
                for b in range(2):
                    moved = placed(4 * i + h, 2, b, b)
                    at = slice(b * BLOCK, (b + 1) * BLOCK)
                    target[first + h, at, :] = moved[:, :128]
                    target[first + h + 1, at, :] = moved[:, 128:]
        else:
            for b in range(2):
                moved = placed(16, 2, b, b)
                at = slice((b + 1) * BLOCK, (b + 2) * BLOCK)
                ks[at, :] = moved[:, :128]
                vs[at, :] = moved[:, 128:]
            ks[:BLOCK, :] = placed(18, 1, 0, 2)
            vs[:BLOCK, :] = placed(18, 1, 1, 3)
            kt[...] = dot_nt(onehot(iota((128, 128), 0), iota((128, 128), 1)), ks[...]).astype(BF16)

    def over(first, n):
        length = n * 128
        for ib in [first + k for k in range(QB)]:
            rows = pl.ds(pl.multiple_of(ib * 128, 128), 128)
            query_doc = doc_ref[pl.ds(8 * pair + ib, 1), :].astype(F32)
            window = pl.ds(pl.multiple_of((ib + 5 - n) * 128, 128), length)
            keys, values, keys_t = ks[window, :], vs[window, :], kt[:, window]
            later = iota((length, 128), 0) - iota((length, 128), 1) > length - 128
            bias = jnp.where((doc_t[window, :] == query_doc) & ~later, 0.0, NEG)
            bias = jnp.concatenate([bias] * PER, axis=1)
            all_weights, all_dscore, all_query, all_grad = [], [], [], []
            for h in range(0, WIDTH, PER):
                query = jnp.concatenate([qs[h + k, rows, :] for k in range(PER)], axis=0)
                grad = jnp.concatenate([ws[h + k, rows, :] for k in range(PER)], axis=0)
                score = dot_nt(keys, query) * (SCALE * LOG2E) + bias
                prob = jnp.exp2(score - jnp.max(score, axis=0, keepdims=True))
                prob = prob * (1.0 / jnp.sum(prob, axis=0, keepdims=True))
                weights = prob.astype(BF16)
                dprob = dot_nt(values, grad)
                delta = jnp.sum(weights.astype(F32) * dprob, axis=0, keepdims=True)
                dscore = (prob * SCALE * (dprob - delta)).astype(BF16)
                dq = dot(keys_t, dscore).astype(BF16)
                for k in range(PER):
                    dq_t[h + k, :, rows] = dq[:, k * 128 : (k + 1) * 128]
                all_weights.append(weights)
                all_dscore.append(dscore)
                all_query.append(query)
                all_grad.append(grad)
            dv_acc[window, :] += dot(
                jnp.concatenate(all_weights, axis=1), jnp.concatenate(all_grad, axis=0)
            )
            dk_acc[window, :] += dot(
                jnp.concatenate(all_dscore, axis=1), jnp.concatenate(all_query, axis=0)
            )

    def query_blocks(i, carry):
        first = i * QB
        count = counts[first]
        for k in range(1, QB):
            count = jnp.maximum(count, counts[first + k])
        pl.when(count <= 2)(lambda: over(first, 2))
        pl.when(count == 3)(lambda: over(first, 3))
        pl.when(count >= 4)(lambda: over(first, 5))
        return carry

    lax.fori_loop(0, 8 // QB, query_blocks, 0)

    def woven(one, two):
        a, b = one.reshape(64, 8, 128), two.reshape(64, 8, 128)
        rows = jnp.concatenate([jnp.where(upper, a, b), jnp.where(upper, b, a)], axis=1)
        return rows.reshape(1024, 128)

    def rounded(b):
        at = slice(b * BLOCK, (b + 1) * BLOCK)
        return dk_acc[at, :].astype(BF16), dv_acc[at, :].astype(BF16)

    both = [dot(to_src[b], jnp.concatenate(rounded(b + 1), axis=1)) for b in range(2)]
    halo_key, halo_value = rounded(0)
    tiles = [woven(both[0][:, i * 128 : (i + 1) * 128], both[1][:, i * 128 : (i + 1) * 128]) for i in range(2)]
    tiles.append(woven(dot(to_src[2], halo_key), dot(to_src[3], halo_value)))
    tiles_to(out_ref, 8 * WIDTH, tiles)
    for h in range(0, WIDTH, 2):
        both = [
            dot_nt(
                to_src[b],
                jnp.concatenate([dq_t[h + i, :, b * BLOCK : (b + 1) * BLOCK] for i in range(2)], axis=0),
            )
            for b in range(2)
        ]
        tiles = [woven(both[0][:, i * 128 : (i + 1) * 128], both[1][:, i * 128 : (i + 1) * 128]) for i in range(2)]
        tiles_to(out_ref, 8 * h, tiles)


def return_kernel(
    me_ref, place_hbm, in_ref, dq_hbm, dk_hbm, dv_hbm, place_ref, dq_ref, dk_ref, dv_ref, sems, small
):
    place_copy = fetch_place(place_hbm, place_ref, me_ref[0], small.at[0])

    def copy_dq(g):
        at = slice(g * WIDTH * D, (g + 1) * WIDTH * D)
        return pltpu.make_async_copy(dq_ref.at[:, at], dq_hbm.at[:, at], sems.at[g])

    place_copy.wait()

    def column(code):
        return jnp.transpose(jnp.broadcast_to(code.astype(F32), (128, 128))).astype(jnp.int32)

    def wide(code, tile):
        return lax.shift_right_logical(code, 3) * 16 + (code & 7) + 8 * tile

    own_c, key_c, value_c = [column(c) for c in token_codes(place_ref, me_ref[0])]
    own = jnp.concatenate(
        [
            jnp.concatenate([onehot(iota((128, 128), 1) + 128 * at, wide(own_c, i)) for at in range(2)], axis=1)
            for i in range(2)
        ],
        axis=0,
    )
    keys, values = onehot(iota((128, 128), 1), key_c), onehot(iota((128, 128), 1), value_c)
    for g in range(GROUPS):

        def pair_of(tile):
            return in_ref[:, g, 8 * tile : 8 * tile + 16, :].reshape(256, 128)

        for h in range(0, WIDTH, 4):
            moved = dot(own, jnp.concatenate([pair_of(h), pair_of(h + 2)], axis=1)).astype(BF16)
            for i, (a, b) in enumerate(((0, 0), (1, 0), (0, 1), (1, 1))):
                at = (g * WIDTH + h + i) * D
                dq_ref[:, at : at + D] = moved[a * 128 : (a + 1) * 128, b * 128 : (b + 1) * 128]
        moved = dot(own, pair_of(WIDTH))
        halo = in_ref[:, g, 8 * WIDTH + 16 :, :].astype(F32).reshape(128, 128).astype(BF16)
        narrow = slice(g * D, (g + 1) * D)
        dk_ref[:, narrow] = (moved[:128] + dot(keys, halo)).astype(BF16)
        dv_ref[:, narrow] = (moved[128:] + dot(values, halo)).astype(BF16)
        copy_dq(g).start()
    last = [
        pltpu.make_async_copy(dk_ref, dk_hbm, small.at[1]),
        pltpu.make_async_copy(dv_ref, dv_hbm, small.at[2]),
    ]
    for copy in last:
        copy.start()
    for g in range(GROUPS):
        copy_dq(g).wait()
    for copy in last:
        copy.wait()


SMEM = pl.BlockSpec(memory_space=pltpu.SMEM)
ANY = pl.BlockSpec(memory_space=pl.ANY)
VMEM = pl.BlockSpec(memory_space=pltpu.VMEM)


def params(mib):
    return pltpu.CompilerParams(vmem_limit_bytes=mib * 1024 * 1024)


def exchanged(rows):
    return lax.all_to_all(rows, ("ctx", "head"), split_axis=0, concat_axis=0, tiled=True)


def sent(me, place2, advantage, query, grad_out, key, value):
    out = pl.pallas_call(
        send_kernel,
        in_specs=[SMEM] + [ANY] * 6,
        out_specs=ANY,
        out_shape=jax.ShapeDtypeStruct((PAIRS, GROUPS, SEND_ROWS, 128), BF16),
        scratch_shapes=[
            pltpu.VMEM((8, 128), jnp.int32),
            pltpu.VMEM((1, 128), F32),
            pltpu.VMEM((128, GROUPS * WIDTH * D), BF16),
            pltpu.VMEM((128, GROUPS * WIDTH * D), BF16),
            pltpu.VMEM((128, GROUPS * D), BF16),
            pltpu.VMEM((128, GROUPS * D), BF16),
            pltpu.VMEM((PAIRS, GROUPS, SEND_ROWS, 128), BF16),
            pltpu.SemaphoreType.DMA((3, GROUPS)),
            pltpu.SemaphoreType.DMA((4,)),
        ],
        compiler_params=params(SEND_MIB),
        name="to_blocks",
    )(me, place2, advantage.reshape(1, 128), query, grad_out, key, value)
    return out.reshape(PAIRS * GROUPS, SEND_ROWS, 128)


def shards(query, key, value, grad_out, advantage, place, segment):
    me = (lax.axis_index("ctx") * 4 + lax.axis_index("head")).astype(jnp.int32).reshape(1)
    place2 = place.reshape(128, 128)
    doc2 = segment.reshape(128, 128)
    arrived = exchanged(sent(me, place2, advantage, query, grad_out, key, value))

    maps = pltpu.VMEM((4, BLOCK, BLOCK), BF16)
    heads = pltpu.VMEM((WIDTH, 2 * BLOCK, D), BF16)
    gradients = pl.pallas_call(
        attend_kernel,
        in_specs=[SMEM, ANY, ANY, VMEM],
        out_specs=VMEM,
        out_shape=jax.ShapeDtypeStruct((128, BACK_ROWS, 128), BF16),
        scratch_shapes=[
            pltpu.VMEM((128, 128), jnp.int32),
            pltpu.VMEM((128, 128), jnp.int32),
            maps,
            maps,
            pltpu.VMEM((4, BLOCK, 128), F32),
            pltpu.VMEM((19, 2, BLOCK, 128), BF16),
            heads,
            heads,
            pltpu.VMEM((SPAN, D), BF16),
            pltpu.VMEM((SPAN, D), BF16),
            pltpu.VMEM((D, SPAN), BF16),
            pltpu.VMEM((SPAN, 128), F32),
            pltpu.VMEM((WIDTH, D, 2 * BLOCK), BF16),
            pltpu.VMEM((SPAN, D), F32),
            pltpu.VMEM((SPAN, D), F32),
            pltpu.SMEM((8,), jnp.int32),
            pltpu.SemaphoreType.DMA((2,)),
        ],
        compiler_params=params(ATTEND_MIB),
        name="attend",
    )(me, place2, doc2, arrived)

    back = exchanged(gradients)
    rows = BACK_ROWS
    wide = (128, GROUPS * WIDTH * D)
    narrow = (128, GROUPS * D)
    return pl.pallas_call(
        return_kernel,
        in_specs=[SMEM, ANY, VMEM],
        out_specs=[ANY] * 3,
        out_shape=[jax.ShapeDtypeStruct(x, BF16) for x in (wide, narrow, narrow)],
        scratch_shapes=[
            pltpu.VMEM((8, 128), jnp.int32),
            pltpu.VMEM(wide, BF16),
            pltpu.VMEM(narrow, BF16),
            pltpu.VMEM(narrow, BF16),
            pltpu.SemaphoreType.DMA((GROUPS,)),
            pltpu.SemaphoreType.DMA((3,)),
        ],
        compiler_params=params(RETURN_MIB),
        name="to_rows",
    )(me, place2, back.reshape(PAIRS, GROUPS, rows, 128))


def solution(mesh):
    spec = P(("ctx", "head"), None)
    in_specs = (spec, spec, spec, spec, P(("ctx", "head")), P(), P())
    return jax.shard_map(
        shards, mesh=mesh, in_specs=in_specs, out_specs=(spec, spec, spec), check_vma=False
    )
```

```python
import functools

import jax
import jax.numpy as jnp
from jax import lax
from jax.experimental import pallas as pl
from jax.experimental.pallas import tpu as pltpu
from jax.sharding import PartitionSpec as P

GROUPS = 8
WIDTH = 8
D = 128
BLOCK = 512
PAIRS = 16
SPAN = 3 * BLOCK
SCALE = D ** (-0.5)
LOG2E = 1.4426950408889634
NEG = -1e30
F32 = jnp.float32
BF16 = jnp.bfloat16

SEND_ROWS = 8 * (2 * WIDTH + 3)
BACK_ROWS = 8 * (WIDTH + 3)
SEND_MIB, ATTEND_MIB, RETURN_MIB = 56, 38, 20
AHEAD = 3
PER = 8
WINDOWS = (3, 4, 5, 6, 8, 10)
QB = 1
IN_ORDER = (4, 0, 1, 2, 3)


def iota(shape, dim):
    return lax.broadcasted_iota(jnp.int32, shape, dim)


def dot(a, b):
    return jnp.dot(a, b, preferred_element_type=F32)


def dot_tn(a, b):
    return lax.dot_general(a, b, (((0,), (0,)), ((), ())), preferred_element_type=F32)


def dot_nt(a, b):
    return lax.dot_general(a, b, (((1,), (1,)), ((), ())), preferred_element_type=F32)


def onehot(index, code):
    return (index == code).astype(F32).astype(BF16)


def token_codes(place_ref, me):
    row = place_ref[pl.ds(me & 7, 1), :]
    dest = lax.shift_right_logical(row, 9)
    across = jnp.broadcast_to(dest.astype(F32), (128, 128))
    before = (across == jnp.transpose(across)) & (iota((128, 128), 0) < iota((128, 128), 1))
    rank = jnp.sum(before.astype(F32), axis=0, keepdims=True).astype(jnp.int32)
    pair, half, odd = lax.shift_right_logical(dest, 1), dest & 1, me & 1
    own = pair * 8 + (half ^ odd) * 4 + rank
    later = (half == 1) & (pair < PAIRS - 1)
    halo_key = jnp.where(later, pair * 8 + 8 + odd * 4 + rank, -1)
    halo_value = jnp.where(later, pair * 8 + 8 + (1 - odd) * 4 + rank, -1)
    return own, halo_key, halo_value


def tiles_to(out_ref, start, tiles):
    n = out_ref.shape[0]
    for i in range(0, len(tiles), 2):
        part = [t.reshape(n, 8, 128) for t in tiles[i : i + 2]]
        part = jnp.concatenate(part, axis=1) if len(part) == 2 else part[0]
        at = start + 8 * i
        out_ref[:, at : at + part.shape[1], :] = part.astype(BF16)


def fetch_place(place_hbm, place_ref, me, sem):
    first = pl.multiple_of(lax.shift_right_logical(me, 3) * 8, 8)
    copy = pltpu.make_async_copy(place_hbm.at[pl.ds(first, 8), :], place_ref, sem)
    copy.start()
    return copy


def send_kernel(
    me_ref, place_hbm, adv_hbm, q_hbm, g_hbm, k_hbm, v_hbm, out_hbm,
    place_ref, adv_ref, q_ref, g_ref, k_ref, v_ref, out_ref, sems, small,
):
    place_copy = fetch_place(place_hbm, place_ref, me_ref[0], small.at[0])
    adv_copy = pltpu.make_async_copy(adv_hbm, adv_ref, small.at[1])
    adv_copy.start()
    whole = [
        pltpu.make_async_copy(k_hbm, k_ref, small.at[2]),
        pltpu.make_async_copy(v_hbm, v_ref, small.at[3]),
    ]

    def copies_in(g):
        at = slice(g * WIDTH * D, (g + 1) * WIDTH * D)
        return [
            pltpu.make_async_copy(source.at[:, at], into.at[:, at], sems.at[i, g])
            for i, (source, into) in enumerate(((q_hbm, q_ref), (g_hbm, g_ref)))
        ]

    def copy_out(g):
        return pltpu.make_async_copy(out_ref.at[:, g], out_hbm.at[:, g], sems.at[2, g])

    for g in range(AHEAD):
        for copy in copies_in(g) + (whole if g == 0 else []):
            copy.start()
    place_copy.wait()
    adv_copy.wait()
    rows = iota((128, 128), 0)
    own, halo_k, halo_v = [onehot(rows, code) for code in token_codes(place_ref, me_ref[0])]
    weight = jnp.transpose(jnp.broadcast_to(adv_ref[...], (128, 128)))
    for g in range(GROUPS):
        for copy in copies_in(g) + (whole if g == 0 else []):
            copy.wait()
        if g + AHEAD < GROUPS:
            for copy in copies_in(g + AHEAD):
                copy.start()
        wide = slice(g * WIDTH * D, (g + 1) * WIDTH * D)
        narrow = slice(g * D, (g + 1) * D)
        grad = g_ref[:, wide]
        grad = jnp.concatenate(
            [(grad[:, h * D : (h + 1) * D].astype(F32) * weight).astype(BF16) for h in range(WIDTH)], axis=1
        )
        tiles = []
        for block in (q_ref[:, wide], grad):
            moved = dot(own, block)
            tiles += [moved[:, h * D : (h + 1) * D] for h in range(WIDTH)]
        key, value = k_ref[:, narrow], v_ref[:, narrow]
        tiles += [dot(own, key), dot(own, value), dot(halo_k, key) + dot(halo_v, value)]
        tiles_to(out_ref.at[:, g], 0, tiles)
        copy_out(g).start()
    for g in range(GROUPS):
        copy_out(g).wait()


def source_maps(place, block, spread_ref, gather_ref, column):
    own = lax.shift_right_logical(place, 9) == block
    member = own.astype(F32)
    earlier = onehot(jnp.int32(1), (iota((128, 128), 0) < iota((128, 128), 1)).astype(jnp.int32))
    rank = dot(member.astype(BF16), earlier)
    picked = jnp.where(own, (place - block * BLOCK + 1).astype(F32), 0.0)
    for r in range(4):
        part = jnp.sum(jnp.where(rank == r, picked, 0.0), axis=1, keepdims=True) - 1.0
        column[pl.ds(r, 128, stride=4), :] = jnp.broadcast_to(part, (128, 128))
    for b in range(4):
        at = slice(b * 128, (b + 1) * 128)
        whole = column[at, :]
        gather_ref[at, :] = jnp.concatenate(
            [onehot(iota((128, 128), 1) + 128 * c, whole.astype(jnp.int32)) for c in range(4)], axis=1
        )
        row = jnp.transpose(whole)[0:1, :].astype(jnp.int32)
        spread_ref[:, at] = onehot(iota((BLOCK, 128), 0), row)


def attend_kernel(
    me_ref, place_ref, doc_ref, in_ref, out_ref,
    to_pos, to_src, column, arrived, qs, ws, ks, vs, doc_t, dq_t, dk_acc, dv_acc, counts,
):
    pair = lax.shift_right_logical(me_ref[0], 3)
    place = place_ref[...]
    even = (iota((128, 128), 0) & 1) == 0
    place_f = place.astype(F32)
    swapped = jnp.where(even, pltpu.roll(place_f, 127, 0), pltpu.roll(place_f, 1, 0)).astype(jnp.int32)
    for i, (rows, block) in enumerate(
        ((place, 2 * pair), (swapped, 2 * pair + 1), (place, 2 * pair - 1), (swapped, 2 * pair - 1))
    ):
        source_maps(rows, block, to_pos.at[i], to_src.at[i], column.at[i])

    docs = doc_ref[...]
    block_at = iota((128, 128), 0)
    last = (iota((128, 128), 1) & 63) == 63
    for ib in range(8):
        block = 8 * pair + ib
        first_doc = doc_ref[pl.ds(block, 1), :][:, 0:1]
        near = last & (block_at < block) & (block_at >= block - 4) & (docs >= first_doc)
        counts[ib] = 2 + jnp.sum(near.astype(F32)).astype(jnp.int32)
    for b in range(12):
        at = 8 * pair - 4 + b
        doc = doc_ref[pl.ds(jnp.maximum(at, 0), 1), :].astype(F32)
        doc = jnp.where(at >= 0, doc, -2.0)
        doc_t[b * 128 : (b + 1) * 128, :] = jnp.transpose(jnp.broadcast_to(doc, (128, 128)))
    dk_acc[...] = jnp.zeros_like(dk_acc)
    dv_acc[...] = jnp.zeros_like(dv_acc)

    upper = iota((64, 8, 128), 1) < 4

    def halves(tile):
        rows = in_ref[:, 8 * tile : 8 * tile + 8, :].astype(F32).reshape(64, 16, 128)
        a, b = rows[:, :8], rows[:, 8:]
        return (
            jnp.where(upper, a, b).reshape(BLOCK, 128).astype(BF16),
            jnp.where(upper, b, a).reshape(BLOCK, 128).astype(BF16),
        )

    def placed(t, count, half, map_at):
        both = jnp.concatenate([arrived[t + i, half] for i in range(count)], axis=1)
        return dot(to_pos[map_at], both).astype(BF16)

    for i in IN_ORDER:
        tiles = range(4 * i, min(4 * i + 4, 19))
        for t in tiles:
            arrived[t, 0], arrived[t, 1] = halves(t)
        if i < 4:
            target, first = (qs, 4 * i) if i < 2 else (ws, 4 * i - 8)
            for h in range(0, 4, 2):
                for b in range(2):
                    moved = placed(4 * i + h, 2, b, b)
                    at = slice(b * BLOCK, (b + 1) * BLOCK)
                    target[first + h, at, :] = moved[:, :128]
                    target[first + h + 1, at, :] = moved[:, 128:]
        else:
            for b in range(2):
                moved = placed(16, 2, b, b)
                at = slice((b + 1) * BLOCK, (b + 2) * BLOCK)
                ks[at, :] = moved[:, :128]
                vs[at, :] = moved[:, 128:]
            ks[:BLOCK, :] = placed(18, 1, 0, 2)
            vs[:BLOCK, :] = placed(18, 1, 1, 3)

    def over(first, n):
        length = n * 64
        for ib in [first + k for k in range(QB)]:
            rows = pl.ds(pl.multiple_of(ib * 128, 128), 128)
            query_doc = doc_ref[pl.ds(8 * pair + ib, 1), :].astype(F32)
            window = pl.ds(pl.multiple_of((ib + 5) * 128 - length, 64), length)
            keys, values = ks[window, :], vs[window, :]
            later = iota((length, 128), 0) - iota((length, 128), 1) > length - 128
            bias = jnp.where((doc_t[window, :] == query_doc) & ~later, 0.0, NEG)
            bias = jnp.concatenate([bias] * PER, axis=1)
            all_weights, all_dscore, all_query, all_grad = [], [], [], []
            for h in range(0, WIDTH, PER):
                query = jnp.concatenate([qs[h + k, rows, :] for k in range(PER)], axis=0)
                grad = jnp.concatenate([ws[h + k, rows, :] for k in range(PER)], axis=0)
                score = dot_nt(keys, query) * (SCALE * LOG2E) + bias
                prob = jnp.exp2(score - jnp.max(score, axis=0, keepdims=True))
                prob = prob * (1.0 / jnp.sum(prob, axis=0, keepdims=True))
                weights = prob.astype(BF16)
                dprob = dot_nt(values, grad)
                delta = jnp.sum(weights.astype(F32) * dprob, axis=0, keepdims=True)
                dscore = (prob * SCALE * (dprob - delta)).astype(BF16)
                dq = dot_tn(keys, dscore).astype(BF16)
                for k in range(PER):
                    dq_t[h + k, :, rows] = dq[:, k * 128 : (k + 1) * 128]
                all_weights.append(weights)
                all_dscore.append(dscore)
                all_query.append(query)
                all_grad.append(grad)
            dv_acc[window, :] += dot(
                jnp.concatenate(all_weights, axis=1), jnp.concatenate(all_grad, axis=0)
            )
            dk_acc[window, :] += dot(
                jnp.concatenate(all_dscore, axis=1), jnp.concatenate(all_query, axis=0)
            )

    def query_blocks(i, carry):
        first = i * QB
        count = counts[first]
        for k in range(1, QB):
            count = jnp.maximum(count, counts[first + k])
        for low, n in zip((0,) + WINDOWS, WINDOWS):
            pl.when((count > low) & (count <= n))(functools.partial(over, first, n))
        return carry

    lax.fori_loop(0, 8 // QB, query_blocks, 0)

    def woven(one, two):
        a, b = one.reshape(64, 8, 128), two.reshape(64, 8, 128)
        rows = jnp.concatenate([jnp.where(upper, a, b), jnp.where(upper, b, a)], axis=1)
        return rows.reshape(1024, 128)

    def rounded(b):
        at = slice(b * BLOCK, (b + 1) * BLOCK)
        return dk_acc[at, :].astype(BF16), dv_acc[at, :].astype(BF16)

    both = [dot(to_src[b], jnp.concatenate(rounded(b + 1), axis=1)) for b in range(2)]
    halo_key, halo_value = rounded(0)
    tiles = [woven(both[0][:, i * 128 : (i + 1) * 128], both[1][:, i * 128 : (i + 1) * 128]) for i in range(2)]
    tiles.append(woven(dot(to_src[2], halo_key), dot(to_src[3], halo_value)))
    tiles_to(out_ref, 8 * WIDTH, tiles)
    for h in range(0, WIDTH, 2):
        both = [
            dot_nt(
                to_src[b],
                jnp.concatenate([dq_t[h + i, :, b * BLOCK : (b + 1) * BLOCK] for i in range(2)], axis=0),
            )
            for b in range(2)
        ]
        tiles = [woven(both[0][:, i * 128 : (i + 1) * 128], both[1][:, i * 128 : (i + 1) * 128]) for i in range(2)]
        tiles_to(out_ref, 8 * h, tiles)


def return_kernel(
    me_ref, place_hbm, in_ref, dq_hbm, dk_hbm, dv_hbm, place_ref, dq_ref, dk_ref, dv_ref, sems, small
):
    place_copy = fetch_place(place_hbm, place_ref, me_ref[0], small.at[0])

    def copy_dq(g):
        at = slice(g * WIDTH * D, (g + 1) * WIDTH * D)
        return pltpu.make_async_copy(dq_ref.at[:, at], dq_hbm.at[:, at], sems.at[g])

    place_copy.wait()

    def column(code):
        return jnp.transpose(jnp.broadcast_to(code.astype(F32), (128, 128))).astype(jnp.int32)

    def wide(code, tile):
        return lax.shift_right_logical(code, 3) * 16 + (code & 7) + 8 * tile

    own_c, key_c, value_c = [column(c) for c in token_codes(place_ref, me_ref[0])]
    own = jnp.concatenate(
        [
            jnp.concatenate([onehot(iota((128, 128), 1) + 128 * at, wide(own_c, i)) for at in range(2)], axis=1)
            for i in range(2)
        ],
        axis=0,
    )
    keys, values = onehot(iota((128, 128), 1), key_c), onehot(iota((128, 128), 1), value_c)
    for g in range(GROUPS):

        def pair_of(tile):
            return in_ref[:, g, 8 * tile : 8 * tile + 16, :].reshape(256, 128)

        for h in range(0, WIDTH, 4):
            moved = dot(own, jnp.concatenate([pair_of(h), pair_of(h + 2)], axis=1)).astype(BF16)
            for i, (a, b) in enumerate(((0, 0), (1, 0), (0, 1), (1, 1))):
                at = (g * WIDTH + h + i) * D
                dq_ref[:, at : at + D] = moved[a * 128 : (a + 1) * 128, b * 128 : (b + 1) * 128]
        moved = dot(own, pair_of(WIDTH))
        halo = in_ref[:, g, 8 * WIDTH + 16 :, :].astype(F32).reshape(128, 128).astype(BF16)
        narrow = slice(g * D, (g + 1) * D)
        dk_ref[:, narrow] = (moved[:128] + dot(keys, halo)).astype(BF16)
        dv_ref[:, narrow] = (moved[128:] + dot(values, halo)).astype(BF16)
        copy_dq(g).start()
    last = [
        pltpu.make_async_copy(dk_ref, dk_hbm, small.at[1]),
        pltpu.make_async_copy(dv_ref, dv_hbm, small.at[2]),
    ]
    for copy in last:
        copy.start()
    for g in range(GROUPS):
        copy_dq(g).wait()
    for copy in last:
        copy.wait()


SMEM = pl.BlockSpec(memory_space=pltpu.SMEM)
ANY = pl.BlockSpec(memory_space=pl.ANY)
VMEM = pl.BlockSpec(memory_space=pltpu.VMEM)


def params(mib):
    return pltpu.CompilerParams(vmem_limit_bytes=mib * 1024 * 1024)


def exchanged(rows):
    return lax.all_to_all(rows, ("ctx", "head"), split_axis=0, concat_axis=0, tiled=True)


def sent(me, place2, advantage, query, grad_out, key, value):
    out = pl.pallas_call(
        send_kernel,
        in_specs=[SMEM] + [ANY] * 6,
        out_specs=ANY,
        out_shape=jax.ShapeDtypeStruct((PAIRS, GROUPS, SEND_ROWS, 128), BF16),
        scratch_shapes=[
            pltpu.VMEM((8, 128), jnp.int32),
            pltpu.VMEM((1, 128), F32),
            pltpu.VMEM((128, GROUPS * WIDTH * D), BF16),
            pltpu.VMEM((128, GROUPS * WIDTH * D), BF16),
            pltpu.VMEM((128, GROUPS * D), BF16),
            pltpu.VMEM((128, GROUPS * D), BF16),
            pltpu.VMEM((PAIRS, GROUPS, SEND_ROWS, 128), BF16),
            pltpu.SemaphoreType.DMA((3, GROUPS)),
            pltpu.SemaphoreType.DMA((4,)),
        ],
        compiler_params=params(SEND_MIB),
        name="to_blocks",
    )(me, place2, advantage.reshape(1, 128), query, grad_out, key, value)
    return out.reshape(PAIRS * GROUPS, SEND_ROWS, 128)


def shards(query, key, value, grad_out, advantage, place, segment):
    me = (lax.axis_index("ctx") * 4 + lax.axis_index("head")).astype(jnp.int32).reshape(1)
    place2 = place.reshape(128, 128)
    doc2 = segment.reshape(128, 128)
    arrived = exchanged(sent(me, place2, advantage, query, grad_out, key, value))

    maps = pltpu.VMEM((4, BLOCK, BLOCK), BF16)
    heads = pltpu.VMEM((WIDTH, 2 * BLOCK, D), BF16)
    gradients = pl.pallas_call(
        attend_kernel,
        in_specs=[SMEM, VMEM, VMEM, VMEM],
        out_specs=VMEM,
        out_shape=jax.ShapeDtypeStruct((128, BACK_ROWS, 128), BF16),
        scratch_shapes=[
            maps,
            maps,
            pltpu.VMEM((4, BLOCK, 128), F32),
            pltpu.VMEM((19, 2, BLOCK, 128), BF16),
            heads,
            heads,
            pltpu.VMEM((SPAN, D), BF16),
            pltpu.VMEM((SPAN, D), BF16),
            pltpu.VMEM((SPAN, 128), F32),
            pltpu.VMEM((WIDTH, D, 2 * BLOCK), BF16),
            pltpu.VMEM((SPAN, D), F32),
            pltpu.VMEM((SPAN, D), F32),
            pltpu.SMEM((8,), jnp.int32),
        ],
        compiler_params=params(ATTEND_MIB),
        name="attend",
    )(me, place2, doc2, arrived)

    back = exchanged(gradients)
    rows = BACK_ROWS
    wide = (128, GROUPS * WIDTH * D)
    narrow = (128, GROUPS * D)
    return pl.pallas_call(
        return_kernel,
        in_specs=[SMEM, ANY, VMEM],
        out_specs=[ANY] * 3,
        out_shape=[jax.ShapeDtypeStruct(x, BF16) for x in (wide, narrow, narrow)],
        scratch_shapes=[
            pltpu.VMEM((8, 128), jnp.int32),
            pltpu.VMEM(wide, BF16),
            pltpu.VMEM(narrow, BF16),
            pltpu.VMEM(narrow, BF16),
            pltpu.SemaphoreType.DMA((GROUPS,)),
            pltpu.SemaphoreType.DMA((3,)),
        ],
        compiler_params=params(RETURN_MIB),
        name="to_rows",
    )(me, place2, back.reshape(PAIRS, GROUPS, rows, 128))


def solution(mesh):
    spec = P(("ctx", "head"), None)
    in_specs = (spec, spec, spec, spec, P(("ctx", "head")), P(), P())
    return jax.shard_map(
        shards, mesh=mesh, in_specs=in_specs, out_specs=(spec, spec, spec), check_vma=False
    )
```

```python
import functools

import jax
import jax.numpy as jnp
from jax import lax
from jax.experimental import pallas as pl
from jax.experimental.pallas import tpu as pltpu
from jax.sharding import PartitionSpec as P

GROUPS = 8
WIDTH = 8
D = 128
BLOCK = 512
PAIRS = 16
SPAN = 3 * BLOCK
SCALE = D ** (-0.5)
LOG2E = 1.4426950408889634
NEG = -1e30
F32 = jnp.float32
BF16 = jnp.bfloat16

SEND_ROWS = 8 * (2 * WIDTH + 3)
BACK_ROWS = 8 * (WIDTH + 3)
SEND_MIB, ATTEND_MIB, RETURN_MIB = 56, 38, 20
AHEAD = 3
PER = 8
WINDOWS = (3, 4, 5, 6, 8, 10)
QB = 1
IN_ORDER = (4, 0, 1, 2, 3)


def iota(shape, dim):
    return lax.broadcasted_iota(jnp.int32, shape, dim)


def dot(a, b):
    return jnp.dot(a, b, preferred_element_type=F32)


def dot_tn(a, b):
    return lax.dot_general(a, b, (((0,), (0,)), ((), ())), preferred_element_type=F32)


def dot_nt(a, b):
    return lax.dot_general(a, b, (((1,), (1,)), ((), ())), preferred_element_type=F32)


def onehot(index, code):
    return (index == code).astype(F32).astype(BF16)


def token_codes(place_ref, me):
    row = place_ref[pl.ds(me & 7, 1), :]
    dest = lax.shift_right_logical(row, 9)
    across = jnp.broadcast_to(dest.astype(F32), (128, 128))
    before = (across == jnp.transpose(across)) & (iota((128, 128), 0) < iota((128, 128), 1))
    rank = jnp.sum(before.astype(F32), axis=0, keepdims=True).astype(jnp.int32)
    pair, half, odd = lax.shift_right_logical(dest, 1), dest & 1, me & 1
    own = pair * 8 + (half ^ odd) * 4 + rank
    later = (half == 1) & (pair < PAIRS - 1)
    halo_key = jnp.where(later, pair * 8 + 8 + odd * 4 + rank, -1)
    halo_value = jnp.where(later, pair * 8 + 8 + (1 - odd) * 4 + rank, -1)
    return own, halo_key, halo_value


def tiles_to(out_ref, start, tiles):
    n = out_ref.shape[0]
    for i in range(0, len(tiles), 2):
        part = [t.reshape(n, 8, 128) for t in tiles[i : i + 2]]
        part = jnp.concatenate(part, axis=1) if len(part) == 2 else part[0]
        at = start + 8 * i
        out_ref[:, at : at + part.shape[1], :] = part.astype(BF16)


def fetch_place(place_hbm, place_ref, me, sem):
    first = pl.multiple_of(lax.shift_right_logical(me, 3) * 8, 8)
    copy = pltpu.make_async_copy(place_hbm.at[pl.ds(first, 8), :], place_ref, sem)
    copy.start()
    return copy


def send_kernel(
    me_ref, place_hbm, adv_hbm, q_hbm, g_hbm, k_hbm, v_hbm, out_hbm,
    place_ref, adv_ref, q_ref, g_ref, k_ref, v_ref, out_ref, sems, small,
):
    place_copy = fetch_place(place_hbm, place_ref, me_ref[0], small.at[0])
    adv_copy = pltpu.make_async_copy(adv_hbm, adv_ref, small.at[1])
    adv_copy.start()
    whole = [
        pltpu.make_async_copy(k_hbm, k_ref, small.at[2]),
        pltpu.make_async_copy(v_hbm, v_ref, small.at[3]),
    ]

    def copies_in(g):
        at = slice(g * WIDTH * D, (g + 1) * WIDTH * D)
        return [
            pltpu.make_async_copy(source.at[:, at], into.at[:, at], sems.at[i, g])
            for i, (source, into) in enumerate(((q_hbm, q_ref), (g_hbm, g_ref)))
        ]

    def copy_out(g):
        return pltpu.make_async_copy(out_ref.at[:, g], out_hbm.at[:, g], sems.at[2, g])

    for g in range(AHEAD):
        for copy in copies_in(g) + (whole if g == 0 else []):
            copy.start()
    place_copy.wait()
    adv_copy.wait()
    rows = iota((128, 128), 0)
    own, halo_k, halo_v = [onehot(rows, code) for code in token_codes(place_ref, me_ref[0])]
    weight = jnp.transpose(jnp.broadcast_to(adv_ref[...], (128, 128)))
    for g in range(GROUPS):
        for copy in copies_in(g) + (whole if g == 0 else []):
            copy.wait()
        if g + AHEAD < GROUPS:
            for copy in copies_in(g + AHEAD):
                copy.start()
        wide = slice(g * WIDTH * D, (g + 1) * WIDTH * D)
        narrow = slice(g * D, (g + 1) * D)
        grad = g_ref[:, wide]
        grad = jnp.concatenate(
            [(grad[:, h * D : (h + 1) * D].astype(F32) * weight).astype(BF16) for h in range(WIDTH)], axis=1
        )
        tiles = []
        for block in (q_ref[:, wide], grad):
            moved = dot(own, block)
            tiles += [moved[:, h * D : (h + 1) * D] for h in range(WIDTH)]
        key, value = k_ref[:, narrow], v_ref[:, narrow]
        tiles += [dot(own, key), dot(own, value), dot(halo_k, key) + dot(halo_v, value)]
        tiles_to(out_ref.at[:, g], 0, tiles)
        copy_out(g).start()
    for g in range(GROUPS):
        copy_out(g).wait()


def source_maps(place, block, spread_ref, gather_ref, column):
    own = lax.shift_right_logical(place, 9) == block
    member = own.astype(F32)
    earlier = onehot(jnp.int32(1), (iota((128, 128), 0) < iota((128, 128), 1)).astype(jnp.int32))
    rank = dot(member.astype(BF16), earlier)
    picked = jnp.where(own, (place - block * BLOCK + 1).astype(F32), 0.0)
    for r in range(4):
        part = jnp.sum(jnp.where(rank == r, picked, 0.0), axis=1, keepdims=True) - 1.0
        column[pl.ds(r, 128, stride=4), :] = jnp.broadcast_to(part, (128, 128))
    for b in range(4):
        at = slice(b * 128, (b + 1) * 128)
        whole = column[at, :]
        gather_ref[at, :] = jnp.concatenate(
            [onehot(iota((128, 128), 1) + 128 * c, whole.astype(jnp.int32)) for c in range(4)], axis=1
        )
        row = jnp.transpose(whole)[0:1, :].astype(jnp.int32)
        spread_ref[:, at] = onehot(iota((BLOCK, 128), 0), row)


def attend_kernel(
    me_ref, place_ref, doc_ref, in_ref, out_ref,
    to_pos, to_src, column, arrived, qs, ws, ks, vs, doc_t, dq_t, dk_acc, dv_acc, counts,
):
    pair = lax.shift_right_logical(me_ref[0], 3)
    place = place_ref[...]
    even = (iota((128, 128), 0) & 1) == 0
    place_f = place.astype(F32)
    swapped = jnp.where(even, pltpu.roll(place_f, 127, 0), pltpu.roll(place_f, 1, 0)).astype(jnp.int32)
    for i, (rows, block) in enumerate(
        ((place, 2 * pair), (swapped, 2 * pair + 1), (place, 2 * pair - 1), (swapped, 2 * pair - 1))
    ):
        source_maps(rows, block, to_pos.at[i], to_src.at[i], column.at[i])

    docs = doc_ref[...]
    block_at = iota((128, 128), 0)
    last = (iota((128, 128), 1) & 63) == 63
    for ib in range(8):
        block = 8 * pair + ib
        first_doc = doc_ref[pl.ds(block, 1), :][:, 0:1]
        near = last & (block_at < block) & (block_at >= block - 4) & (docs >= first_doc)
        counts[ib] = 2 + jnp.sum(near.astype(F32)).astype(jnp.int32)
    for b in range(12):
        at = 8 * pair - 4 + b
        doc = doc_ref[pl.ds(jnp.maximum(at, 0), 1), :].astype(F32)
        doc = jnp.where(at >= 0, doc, -2.0)
        doc_t[b * 128 : (b + 1) * 128, :] = jnp.transpose(jnp.broadcast_to(doc, (128, 128)))
    dk_acc[...] = jnp.zeros_like(dk_acc)
    dv_acc[...] = jnp.zeros_like(dv_acc)

    upper = iota((64, 8, 128), 1) < 4

    def halves(tile):
        rows = in_ref[:, 8 * tile : 8 * tile + 8, :].astype(F32).reshape(64, 16, 128)
        a, b = rows[:, :8], rows[:, 8:]
        return (
            jnp.where(upper, a, b).reshape(BLOCK, 128).astype(BF16),
            jnp.where(upper, b, a).reshape(BLOCK, 128).astype(BF16),
        )

    def placed(t, count, half, map_at):
        both = jnp.concatenate([arrived[t + i, half] for i in range(count)], axis=1)
        return dot(to_pos[map_at], both).astype(BF16)

    for i in IN_ORDER:
        tiles = range(4 * i, min(4 * i + 4, 19))
        for t in tiles:
            arrived[t, 0], arrived[t, 1] = halves(t)
        if i < 4:
            target, first = (qs, 4 * i) if i < 2 else (ws, 4 * i - 8)
            for h in range(0, 4, 2):
                for b in range(2):
                    moved = placed(4 * i + h, 2, b, b)
                    at = slice(b * BLOCK, (b + 1) * BLOCK)
                    target[first + h, at, :] = moved[:, :128]
                    target[first + h + 1, at, :] = moved[:, 128:]
        else:
            for b in range(2):
                moved = placed(16, 2, b, b)
                at = slice((b + 1) * BLOCK, (b + 2) * BLOCK)
                ks[at, :] = moved[:, :128]
                vs[at, :] = moved[:, 128:]
            ks[:BLOCK, :] = placed(18, 1, 0, 2)
            vs[:BLOCK, :] = placed(18, 1, 1, 3)

    def over(first, n):
        length = n * 64
        for ib in [first + k for k in range(QB)]:
            rows = pl.ds(pl.multiple_of(ib * 128, 128), 128)
            query_doc = doc_ref[pl.ds(8 * pair + ib, 1), :].astype(F32)
            window = pl.ds(pl.multiple_of((ib + 5) * 128 - length, 64), length)
            keys, values = ks[window, :], vs[window, :]
            later = iota((length, 128), 0) - iota((length, 128), 1) > length - 128
            bias = jnp.where((doc_t[window, :] == query_doc) & ~later, 0.0, NEG)
            bias = jnp.concatenate([bias] * PER, axis=1)
            all_dscore, all_query = [], []
            for h in range(0, WIDTH, PER):
                query = jnp.concatenate([qs[h + k, rows, :] for k in range(PER)], axis=0)
                grad = jnp.concatenate([ws[h + k, rows, :] for k in range(PER)], axis=0)
                score = dot_nt(keys, query) * (SCALE * LOG2E) + bias
                dprob = dot_nt(values, grad)
                prob = jnp.exp2(score - jnp.max(score, axis=0, keepdims=True))
                prob = prob * (1.0 / jnp.sum(prob, axis=0, keepdims=True))
                weights = prob.astype(BF16)
                dv_acc[window, :] += dot(weights, grad)
                delta = jnp.sum(weights.astype(F32) * dprob, axis=0, keepdims=True)
                dscore = (prob * SCALE * (dprob - delta)).astype(BF16)
                dq = dot_tn(keys, dscore).astype(BF16)
                for k in range(PER):
                    dq_t[h + k, :, rows] = dq[:, k * 128 : (k + 1) * 128]
                all_dscore.append(dscore)
                all_query.append(query)
            dk_acc[window, :] += dot(
                jnp.concatenate(all_dscore, axis=1), jnp.concatenate(all_query, axis=0)
            )

    def query_blocks(i, carry):
        first = i * QB
        count = counts[first]
        for k in range(1, QB):
            count = jnp.maximum(count, counts[first + k])
        for low, n in zip((0,) + WINDOWS, WINDOWS):
            pl.when((count > low) & (count <= n))(functools.partial(over, first, n))
        return carry

    lax.fori_loop(0, 8 // QB, query_blocks, 0)

    def woven(one, two):
        a, b = one.reshape(64, 8, 128), two.reshape(64, 8, 128)
        rows = jnp.concatenate([jnp.where(upper, a, b), jnp.where(upper, b, a)], axis=1)
        return rows.reshape(1024, 128)

    def rounded(b):
        at = slice(b * BLOCK, (b + 1) * BLOCK)
        return dk_acc[at, :].astype(BF16), dv_acc[at, :].astype(BF16)

    both = [dot(to_src[b], jnp.concatenate(rounded(b + 1), axis=1)) for b in range(2)]
    halo_key, halo_value = rounded(0)
    tiles = [woven(both[0][:, i * 128 : (i + 1) * 128], both[1][:, i * 128 : (i + 1) * 128]) for i in range(2)]
    tiles.append(woven(dot(to_src[2], halo_key), dot(to_src[3], halo_value)))
    tiles_to(out_ref, 8 * WIDTH, tiles)
    for h in range(0, WIDTH, 2):
        both = [
            dot_nt(
                to_src[b],
                jnp.concatenate([dq_t[h + i, :, b * BLOCK : (b + 1) * BLOCK] for i in range(2)], axis=0),
            )
            for b in range(2)
        ]
        tiles = [woven(both[0][:, i * 128 : (i + 1) * 128], both[1][:, i * 128 : (i + 1) * 128]) for i in range(2)]
        tiles_to(out_ref, 8 * h, tiles)


def return_kernel(
    me_ref, place_hbm, in_ref, dq_hbm, dk_hbm, dv_hbm, place_ref, dq_ref, dk_ref, dv_ref, sems, small
):
    place_copy = fetch_place(place_hbm, place_ref, me_ref[0], small.at[0])

    def copy_dq(g):
        at = slice(g * WIDTH * D, (g + 1) * WIDTH * D)
        return pltpu.make_async_copy(dq_ref.at[:, at], dq_hbm.at[:, at], sems.at[g])

    place_copy.wait()

    def column(code):
        return jnp.transpose(jnp.broadcast_to(code.astype(F32), (128, 128))).astype(jnp.int32)

    def wide(code, tile):
        return lax.shift_right_logical(code, 3) * 16 + (code & 7) + 8 * tile

    own_c, key_c, value_c = [column(c) for c in token_codes(place_ref, me_ref[0])]
    own = jnp.concatenate(
        [
            jnp.concatenate([onehot(iota((128, 128), 1) + 128 * at, wide(own_c, i)) for at in range(2)], axis=1)
            for i in range(2)
        ],
        axis=0,
    )
    keys, values = onehot(iota((128, 128), 1), key_c), onehot(iota((128, 128), 1), value_c)
    for g in range(GROUPS):

        def pair_of(tile):
            return in_ref[:, g, 8 * tile : 8 * tile + 16, :].reshape(256, 128)

        for h in range(0, WIDTH, 4):
            moved = dot(own, jnp.concatenate([pair_of(h), pair_of(h + 2)], axis=1)).astype(BF16)
            for i, (a, b) in enumerate(((0, 0), (1, 0), (0, 1), (1, 1))):
                at = (g * WIDTH + h + i) * D
                dq_ref[:, at : at + D] = moved[a * 128 : (a + 1) * 128, b * 128 : (b + 1) * 128]
        moved = dot(own, pair_of(WIDTH))
        halo = in_ref[:, g, 8 * WIDTH + 16 :, :].astype(F32).reshape(128, 128).astype(BF16)
        narrow = slice(g * D, (g + 1) * D)
        dk_ref[:, narrow] = (moved[:128] + dot(keys, halo)).astype(BF16)
        dv_ref[:, narrow] = (moved[128:] + dot(values, halo)).astype(BF16)
        copy_dq(g).start()
    last = [
        pltpu.make_async_copy(dk_ref, dk_hbm, small.at[1]),
        pltpu.make_async_copy(dv_ref, dv_hbm, small.at[2]),
    ]
    for copy in last:
        copy.start()
    for g in range(GROUPS):
        copy_dq(g).wait()
    for copy in last:
        copy.wait()


SMEM = pl.BlockSpec(memory_space=pltpu.SMEM)
ANY = pl.BlockSpec(memory_space=pl.ANY)
VMEM = pl.BlockSpec(memory_space=pltpu.VMEM)


def params(mib):
    return pltpu.CompilerParams(vmem_limit_bytes=mib * 1024 * 1024)


def exchanged(rows):
    return lax.all_to_all(rows, ("ctx", "head"), split_axis=0, concat_axis=0, tiled=True)


def sent(me, place2, advantage, query, grad_out, key, value):
    out = pl.pallas_call(
        send_kernel,
        in_specs=[SMEM] + [ANY] * 6,
        out_specs=ANY,
        out_shape=jax.ShapeDtypeStruct((PAIRS, GROUPS, SEND_ROWS, 128), BF16),
        scratch_shapes=[
            pltpu.VMEM((8, 128), jnp.int32),
            pltpu.VMEM((1, 128), F32),
            pltpu.VMEM((128, GROUPS * WIDTH * D), BF16),
            pltpu.VMEM((128, GROUPS * WIDTH * D), BF16),
            pltpu.VMEM((128, GROUPS * D), BF16),
            pltpu.VMEM((128, GROUPS * D), BF16),
            pltpu.VMEM((PAIRS, GROUPS, SEND_ROWS, 128), BF16),
            pltpu.SemaphoreType.DMA((3, GROUPS)),
            pltpu.SemaphoreType.DMA((4,)),
        ],
        compiler_params=params(SEND_MIB),
        name="to_blocks",
    )(me, place2, advantage.reshape(1, 128), query, grad_out, key, value)
    return out.reshape(PAIRS * GROUPS, SEND_ROWS, 128)


def shards(query, key, value, grad_out, advantage, place, segment):
    me = (lax.axis_index("ctx") * 4 + lax.axis_index("head")).astype(jnp.int32).reshape(1)
    place2 = place.reshape(128, 128)
    doc2 = segment.reshape(128, 128)
    arrived = exchanged(sent(me, place2, advantage, query, grad_out, key, value))

    maps = pltpu.VMEM((4, BLOCK, BLOCK), BF16)
    heads = pltpu.VMEM((WIDTH, 2 * BLOCK, D), BF16)
    gradients = pl.pallas_call(
        attend_kernel,
        in_specs=[SMEM, VMEM, VMEM, VMEM],
        out_specs=VMEM,
        out_shape=jax.ShapeDtypeStruct((128, BACK_ROWS, 128), BF16),
        scratch_shapes=[
            maps,
            maps,
            pltpu.VMEM((4, BLOCK, 128), F32),
            pltpu.VMEM((19, 2, BLOCK, 128), BF16),
            heads,
            heads,
            pltpu.VMEM((SPAN, D), BF16),
            pltpu.VMEM((SPAN, D), BF16),
            pltpu.VMEM((SPAN, 128), F32),
            pltpu.VMEM((WIDTH, D, 2 * BLOCK), BF16),
            pltpu.VMEM((SPAN, D), F32),
            pltpu.VMEM((SPAN, D), F32),
            pltpu.SMEM((8,), jnp.int32),
        ],
        compiler_params=params(ATTEND_MIB),
        name="attend",
    )(me, place2, doc2, arrived)

    back = exchanged(gradients)
    rows = BACK_ROWS
    wide = (128, GROUPS * WIDTH * D)
    narrow = (128, GROUPS * D)
    return pl.pallas_call(
        return_kernel,
        in_specs=[SMEM, ANY, VMEM],
        out_specs=[ANY] * 3,
        out_shape=[jax.ShapeDtypeStruct(x, BF16) for x in (wide, narrow, narrow)],
        scratch_shapes=[
            pltpu.VMEM((8, 128), jnp.int32),
            pltpu.VMEM(wide, BF16),
            pltpu.VMEM(narrow, BF16),
            pltpu.VMEM(narrow, BF16),
            pltpu.SemaphoreType.DMA((GROUPS,)),
            pltpu.SemaphoreType.DMA((3,)),
        ],
        compiler_params=params(RETURN_MIB),
        name="to_rows",
    )(me, place2, back.reshape(PAIRS, GROUPS, rows, 128))


def solution(mesh):
    spec = P(("ctx", "head"), None)
    in_specs = (spec, spec, spec, spec, P(("ctx", "head")), P(), P())
    return jax.shard_map(
        shards, mesh=mesh, in_specs=in_specs, out_specs=(spec, spec, spec), check_vma=False
    )
```
